256 devices in a mesh: grp: 2 (over y_hi), band: 16 (over x, y_lo, core), ga: 8 (over z).
Axes of the slice: x: 4, y: 4 (y_hi: 2, y_lo: 2; y = y_hi * 2 + y_lo), z: 8, core: 2. Of those that a mesh axis runs over, the one named last changes fastest.
Arguments:
- occupied: bfloat16 [128, 192, 192], P(('grp', 'band'), 'ga'), may hold values from -4 to 4
- response: bfloat16 [128, 192, 192], P('band', 'ga'), may hold values from -10 to 10
- ground_state: bfloat16 [128, 192, 192], P('band', 'ga'), may hold values from -4 to 4
- field_index: int32 [128], P('band'), may hold values from 0 to 2
- band_energy: float32 [128], P('band'), may hold values from -2 to -0.2
- local_potential: float32 [192, 192], P('ga'), may hold values from -1.5 to 1.5
- field_potential: float32 [3, 192, 192], P(None, 'ga'), may hold values from -6 to 6
- kernel_table: float32 [192, 192], P(None, 'ga'), may hold values from 0.01 to 10
Outputs:
- projector: bfloat16 [128, 192, 192], P('band', 'ga')
- residual: float32 [128, 192, 192], P('band', 'ga')
The draws below stay inside these ranges and needn't reach their ends.
All inputs are finite; a program needn't handle non-finite values.
Results may differ from the reference program's by a relative error of at most 0.006.
Values may be sent and summed in bfloat16 or wider, within the bound.
A program may use at most 64 MiB of HBM per device.

```python
import math
import jax
import jax.numpy as jnp
from jax import lax

G1 = 192
G2 = 192
FIELDS = 3
NOCC = 128
NRESP = 128


def draw_response(key, part):
    key = jax.random.fold_in(key, 5)
    key_common, key_own = jax.random.split(key, 2)
    shape = (NRESP, G1, G2)
    common = jnp.clip(jax.random.normal(key_common, (1, G1, G2), jnp.float32), -4.0, 4.0)
    own = jnp.clip(jax.random.normal(key_own, shape, jnp.float32), -4.0, 4.0)
    return (0.7 * common + 0.7 * own).astype(jnp.bfloat16)


def touch_ends(array, rng, smallest, largest):
    spot = [jax.random.randint(jax.random.fold_in(rng, axis), (), 0, length) for axis, length in enumerate(array.shape)]
    widest = array.shape.index(max(array.shape))
    beside = spot[:widest] + [(spot[widest] + 1) % array.shape[widest]] + spot[widest + 1:]
    return array.at[tuple(spot)].set(smallest).at[tuple(beside)].set(largest)


def level_of(rng, shape, cuts, low, high):
    loudness = 1.0
    for position, blocks in cuts:
        heights = jax.random.uniform(jax.random.fold_in(jax.random.fold_in(rng, 6), position), (blocks,), jnp.float32, low / len(cuts), high / len(cuts))
        loudness = loudness * jnp.repeat(jnp.exp(heights), shape[position] // blocks).reshape((-1,) + (1,) * (len(shape) - 1 - position))
    return loudness


def bell_draw(own_key, dims, scale, most, pieces=(), kind=jnp.bfloat16):
    gain = level_of(own_key, dims, pieces, -0.22, 0.18) if pieces else 1.0
    drawn = jax.random.normal(own_key, dims, jnp.float32) * scale * gain
    return jnp.minimum(jnp.maximum(drawn, -most), most).astype(kind)


def setup_inputs(seed: int = 0) -> dict:
    seeds = jax.random.split(jax.random.key(seed), 9)
    occupied = bell_draw(seeds[0], (NOCC, G1, G2), 1.0, 4.0, ((0, 32), (1, 8)))
    response = draw_response(jax.random.fold_in(seeds[8], 71), 0)
    ground_state = bell_draw(seeds[2], (NRESP, G1, G2), 1.0, 4.0, ((0, 16), (1, 8)))
    field_index = touch_ends(jax.random.randint(seeds[3], (NRESP,), 0, FIELDS), jax.random.fold_in(seeds[3], 1), 0, FIELDS - 1).astype(jnp.int32)
    band_energy = jnp.clip(-2.0 + 1.8 * jax.random.uniform(seeds[4], (NRESP,), jnp.float32) ** level_of(seeds[4], (NRESP,), ((0, 16),), -0.2, 0.2), -2.0, -0.2)
    local_potential = jnp.clip(jax.random.uniform(seeds[5], (G1, G2), jnp.float32, -1.5, 1.5) * level_of(seeds[5], (G1, G2), ((0, 8),), -0.4, 0.0), -1.5, 1.5)
    field_potential = bell_draw(seeds[6], (FIELDS, G1, G2), 1.0, 6.0, ((1, 8),), jnp.float32)
    kernel_table = jnp.clip(jnp.exp(math.log(10.0) - 6.9077553 * jax.random.uniform(seeds[7], (G1, G2), jnp.float32) ** level_of(seeds[7], (G1, G2), ((1, 8),), -0.2, 0.2)), 0.01, 10.0)
    return {"occupied": occupied, "response": response, "ground_state": ground_state, "field_index": field_index, "band_energy": band_energy, "local_potential": local_potential, "field_potential": field_potential, "kernel_table": kernel_table}


EXCHANGE_FRACTION = 0.25

def cosine_table(length):
    rows = lax.broadcasted_iota(jnp.float32, (length, length), 0)
    cols = lax.broadcasted_iota(jnp.float32, (length, length), 1)
    factor = jnp.where(rows == 0, jnp.sqrt(1.0 / length), jnp.sqrt(2.0 / length)).astype(jnp.float32)
    return factor * jnp.cos(jnp.pi * (cols + 0.5) * rows / length)

def settle(values):
    return lax.optimization_barrier(values.astype(jnp.bfloat16)).astype(jnp.float32)

def kernel_apply(density, table_one, table_two, kernel_table):
    first = settle(jnp.einsum('pan,kn->pak', density, table_two))
    second = jnp.einsum('ka,pab->pkb', table_one, first)
    weighted = settle(second * kernel_table)
    third = settle(jnp.einsum('ka,pkb->pab', table_one, weighted))
    return jnp.einsum('pak,kn->pan', third, table_two)

def reference(occupied, response, ground_state, field_index, band_energy, local_potential, field_potential, kernel_table):
    table_one = settle(cosine_table(G1))
    table_two = settle(cosine_table(G2))
    resp_f32 = response.astype(jnp.float32)
    blocks = occupied.reshape(NOCC // 2, 2, G1, G2)

    def visit(total, block):
        block_f32 = block.astype(jnp.float32)
        density = settle(block_f32[:, None] * resp_f32[None]).reshape(2 * NRESP, G1, G2)
        potential = kernel_apply(density, table_one, table_two, kernel_table).reshape(2, NRESP, G1, G2)
        return (total + lax.optimization_barrier(jnp.sum(block_f32[:, None] * potential, axis=0)) / NOCC, None)
    exchange, _ = lax.scan(visit, jnp.zeros((NRESP, G1, G2), jnp.float32), blocks)
    flat_round = settle(exchange).reshape(NRESP, G1 * G2)
    gram = jnp.dot(resp_f32.reshape(NRESP, G1 * G2), flat_round.T, precision=lax.Precision.HIGHEST) / (G1 * G2)
    gram = 0.5 * (gram + gram.T)
    lower = jnp.linalg.cholesky(gram)
    inverse = lax.linalg.triangular_solve(lower, jnp.eye(NRESP, dtype=jnp.float32), left_side=True, lower=True)
    projector = jnp.dot(inverse, flat_round, precision=lax.Precision.HIGHEST).reshape(NRESP, G1, G2).astype(jnp.bfloat16)
    neighbours = jnp.roll(resp_f32, 1, axis=1) + jnp.roll(resp_f32, -1, axis=1)
    neighbours = neighbours + jnp.roll(resp_f32, 1, axis=2) + jnp.roll(resp_f32, -1, axis=2)
    kinetic = 0.5 * (4.0 * resp_f32 - neighbours)
    select = (field_index[:, None] == jnp.arange(FIELDS, dtype=jnp.int32)[None]).astype(jnp.float32)
    perturb = jnp.einsum('rf,fab->rab', select, field_potential, precision=lax.Precision.HIGHEST)
    residual = kinetic + (local_potential[None] - band_energy[:, None, None]) * resp_f32
    residual = residual - EXCHANGE_FRACTION * exchange + perturb * ground_state.astype(jnp.float32)
    return (projector, residual)
```

```python
import functools

import jax
import jax.numpy as jnp
import ml_dtypes
import numpy as np
from jax import lax
from jax.experimental import pallas as pl
from jax.experimental.pallas import tpu as pltpu
from jax.sharding import PartitionSpec as P

EXCHANGE_FRACTION = 0.25
F32, BF16 = jnp.float32, jnp.bfloat16
MESH = pl.DeviceIdType.MESH
N = 192
NZ = 8
SLAB = N // NZ
HALF = N // 2
BANDS = 128


def cosine_table(length):
    rows = np.arange(length, dtype=np.float32)[:, None]
    cols = np.arange(length, dtype=np.float32)[None]
    one, two = np.sqrt(np.float32(1.0 / length)), np.sqrt(np.float32(2.0 / length))
    factor = np.where(rows == 0, one, two).astype(np.float32)
    angle = np.float32(np.pi) * (cols + np.float32(0.5)) * rows / np.float32(length)
    return (factor * np.cos(angle)).astype(ml_dtypes.bfloat16)


def inverse_factor(gram):
    lane = lax.broadcasted_iota(jnp.int32, (8, BANDS), 1)
    sub = lax.broadcasted_iota(jnp.int32, (8, BANDS), 0)
    count = BANDS // 8
    blocks = [gram[8 * i : 8 * i + 8, :] for i in range(count)]
    done = []
    for b in range(count):
        k0 = 8 * b
        inside = (lane >= k0) & (lane < k0 + 8)
        rows = [jnp.broadcast_to(blocks[b][t : t + 1, :], (8, BANDS)) for t in range(8)]
        a = [
            [jnp.broadcast_to(rows[t][:, k0 + s : k0 + s + 1], (8, BANDS)) for s in range(t + 1)]
            for t in range(8)
        ]
        low = [[None] * 8 for _ in range(8)]
        rinv = [None] * 8
        for t in range(8):
            rinv[t] = lax.rsqrt(a[t][t])
            for u in range(t + 1, 8):
                low[u][t] = a[u][t] * rinv[t]
            for u in range(t + 1, 8):
                for s in range(t + 1, u + 1):
                    a[u][s] = a[u][s] - low[u][t] * low[s][t]
        inv = [[None] * 8 for _ in range(8)]
        for s in range(8):
            inv[s][s] = rinv[s]
            for t in range(s + 1, 8):
                acc = low[t][s] * inv[s][s]
                for u in range(s + 1, t):
                    acc = acc + low[t][u] * inv[u][s]
                inv[t][s] = -(acc * rinv[t])
        unit = [
            jnp.where(lane == k0 + t, 1.0, jnp.where(inside, 0.0, rows[t])) for t in range(8)
        ]
        panel = []
        for t in range(8):
            acc = inv[t][0] * unit[0]
            for s in range(1, t + 1):
                acc = acc + inv[t][s] * unit[s]
            panel.append(acc)
        packed = panel[0]
        for t in range(1, 8):
            packed = jnp.where(sub == t, panel[t], packed)
        done.append(jnp.where(lane <= sub + k0, packed, 0.0))
        for i in range(b + 1, count):
            column = [
                jnp.broadcast_to(blocks[i][:, k0 + s : k0 + s + 1], (8, BANDS)) for s in range(8)
            ]
            new = jnp.where(inside, 0.0, blocks[i])
            for t in range(8):
                factor = inv[t][0] * column[0]
                for s in range(1, t + 1):
                    factor = factor + inv[t][s] * column[s]
                new = new - factor * panel[t]
            blocks[i] = new
    return jnp.concatenate(done, axis=0)


def split_bf16(value):
    first = value.astype(BF16)
    rest = value - first.astype(F32)
    second = rest.astype(BF16)
    third = (rest - second.astype(F32)).astype(BF16)
    return [first.astype(F32), second.astype(F32), third.astype(F32)]


def mod4(i):
    return lax.rem(i, 4)


class PlaneGather:
    def __init__(self, place, ref, first, second, sib, got, got_sib):
        self.place, self.ref = place, ref
        self.s_first, self.s_second, self.s_sib = first, second, sib
        self.r_ici, self.r_sib = got, got_sib

    def slot(self, d, e):
        p = self.place
        f, s = mod4(p.f + d), mod4(p.s + e)
        return (1 - p.c) * (4 * s + f) + p.c * (4 * f + s)

    def peer(self, d, e):
        p = self.place
        f, s = mod4(p.f + d), mod4(p.s + e)
        return p.dev((1 - p.c) * f + p.c * s, (1 - p.c) * s + p.c * f, p.z, p.c)

    def copy(self, sl, half, send, recv, device):
        part = self.ref.at[sl, half]
        return pltpu.make_async_remote_copy(
            src_ref=part,
            dst_ref=part,
            send_sem=send,
            recv_sem=recv,
            device_id=device,
            device_id_type=MESH,
        )

    def first_copy(self, d):
        sl = self.slot(0, 0)
        return self.copy(sl, self.place.c, self.s_first.at[d - 1], self.r_ici.at[sl], self.peer(d, 0))

    def second_copy(self, d, e):
        sl = self.slot(d, 0)
        return self.copy(
            sl, self.place.c, self.s_second.at[3 * d + e - 1], self.r_ici.at[sl], self.peer(0, e)
        )

    def sib_copy(self, d, e):
        p = self.place
        sl = self.slot(d, e)
        return self.copy(sl, p.c, self.s_sib.at[4 * d + e], self.r_sib.at[sl], p.sibling)

    def start(self):
        for d in (1, 3, 2):
            self.first_copy(d).start()
        for e in (1, 3, 2):
            self.second_copy(0, e).start()
        self.sib_copy(0, 0).start()

    def forward(self):
        for d in (1, 3, 2):
            sl = self.slot(d, 0)
            self.copy(
                sl, self.place.c, self.s_first.at[0], self.r_ici.at[sl], self.peer(d, 0)
            ).wait_recv()
            for e in (1, 3, 2):
                self.second_copy(d, e).start()
            self.sib_copy(d, 0).start()

    def hand_on(self, e):
        for d in (0, 1, 3, 2):
            sl = self.slot(d, e)
            self.copy(
                sl, self.place.c, self.s_first.at[0], self.r_ici.at[sl], self.peer(0, e)
            ).wait_recv()
            self.sib_copy(d, e).start()

    def wait_sib(self, sl):
        p = self.place
        self.copy(sl, 1 - p.c, self.s_sib.at[0], self.r_sib.at[sl], p.sibling).wait_recv()

    def finish(self):
        for d in (1, 2, 3):
            self.first_copy(d).wait_send()
        for d in range(4):
            for e in (1, 2, 3):
                self.second_copy(d, e).wait_send()
        for d in range(4):
            for e in range(4):
                self.sib_copy(d, e).wait_send()


class Place:
    def __init__(self):
        self.g = lax.axis_index("grp")
        self.b = lax.axis_index("band")
        self.z = lax.axis_index("ga")
        self.x = lax.div(self.b, 4)
        self.y_lo = lax.rem(lax.div(self.b, 2), 2)
        self.c = lax.rem(self.b, 2)
        self.y = 2 * self.g + self.y_lo
        self.f = (1 - self.c) * self.x + self.c * self.y
        self.s = (1 - self.c) * self.y + self.c * self.x
        self.sibling = self.dev(self.x, self.y, self.z, 1 - self.c)

    def dev(self, x, y, z, c):
        return {"grp": lax.div(y, 2), "band": 4 * x + 2 * lax.rem(y, 2) + c, "ga": z}

    def z_peer(self, d, c):
        return self.dev(self.x, self.y, lax.rem(self.z + d, NZ), c)


def remote(src, dst, send, recv, device):
    return pltpu.make_async_remote_copy(
        src_ref=src,
        dst_ref=dst,
        send_sem=send,
        recv_sem=recv,
        device_id=device,
        device_id_type=MESH,
    )


Z_ORDER = (1, 7, 2, 6, 3, 5, 4)


def kernel(
    occ_ref,
    resp_ref,
    ground_ref,
    index_ref,
    energy_ref,
    local_ref,
    field_ref,
    table_ref,
    c_ref,
    ct_ref,
    proj_ref,
    res_ref,
    occ_src,
    occ_got,
    resp_got,
    resp_sib,
    resp_full,
    table_got,
    table,
    halo_src,
    halo_got,
    occ_all,
    resp_all,
    exch_all,
    total,
    rs_src,
    rs_got,
    rows32,
    exch_own,
    exch_wire,
    gram_z,
    gram_xy,
    gram_full,
    spread,
    proj32,
    *sems,
):
    p = Place()
    z, c, x, y, g = p.z, p.c, p.x, p.y, p.g
    sems = list(sems)
    take = lambda: sems.pop(0)
    occ_s, occ_r = take(), take()
    resp_s, resp_r = take(), take()
    sib_s, sib_r = take(), take()
    table_s, table_r = take(), take()
    halo_s, halo_r = take(), take()
    rs_s, rs_r = take(), take()
    gz_s, gz_r = take(), take()
    gx_s, gx_r = take(), take()
    gy_s, gy_r = take(), take()
    occ_gather = PlaneGather(p, occ_all, *[take() for _ in range(5)])
    resp_gather = PlaneGather(p, resp_all, *[take() for _ in range(5)])
    exch_gather = PlaneGather(p, exch_all, *[take() for _ in range(5)])

    barrier = pltpu.get_barrier_semaphore()
    peers = [p.z_peer(d, k) for d in range(1, NZ) for k in (0, 1)]
    peers += [p.sibling]
    peers += [p.dev(mod4(x + d), y, z, c) for d in (1, 2, 3)]
    peers += [p.dev(x, mod4(y + d), z, c) for d in (1, 2, 3)]
    for peer in peers:
        pl.semaphore_signal(barrier, inc=1, device_id=peer, device_id_type=MESH)

    table_got[z] = table_ref[...].T
    for r in range(4):
        occ_src[r] = occ_ref[r].astype(F32)
    for h in range(2):
        pair = [resp_ref[4 * g + 2 * h + r].astype(F32) for r in range(2)]
        resp_got[h, z] = jnp.concatenate(pair, axis=0).astype(BF16)
    edge = [resp_ref[j].astype(F32) for j in range(8)]
    halo_src[0] = jnp.concatenate([e[SLAB - 1 : SLAB] for e in edge], axis=0)
    halo_src[1] = jnp.concatenate([e[0:1] for e in edge], axis=0)
    pl.semaphore_wait(barrier, len(peers))

    half_of_z = lax.div(z, 4)
    quarter = lax.rem(z, 4)

    def occ_out(r):
        return remote(
            occ_src.at[r],
            occ_got.at[quarter],
            occ_s.at[r],
            occ_r.at[quarter],
            p.dev(x, y, 4 * c + r, half_of_z),
        )

    def occ_in(q):
        return remote(
            occ_src.at[q],
            occ_got.at[q],
            occ_s.at[q],
            occ_r.at[q],
            p.dev(x, y, 4 * c + q, half_of_z),
        )

    def mine(r):
        return (half_of_z == c) & (quarter == r)

    for r in range(4):
        @pl.when(jnp.logical_not(mine(r)))
        def _():
            occ_out(r).start()

        @pl.when(mine(r))
        def _():
            occ_got[r] = occ_src[r]

    def table_copy(d):
        return remote(table_got.at[z], table_got.at[z], table_s.at[d - 1], table_r.at[z], p.z_peer(d, c))

    def resp_copy(h, d):
        return remote(
            resp_got.at[h, z],
            resp_got.at[h, z],
            resp_s.at[7 * h + d - 1],
            resp_r.at[8 * h + z],
            p.z_peer(d, c),
        )

    def resp_wait(h, d):
        src = lax.rem(z + d, NZ)
        remote(
            resp_got.at[h, src],
            resp_got.at[h, src],
            resp_s.at[0],
            resp_r.at[8 * h + src],
            p.z_peer(d, c),
        ).wait_recv()

    def sib_resp(h):
        return remote(resp_got.at[h, z], resp_sib.at[h], sib_s.at[h], sib_r.at[h], p.sibling)

    def halo_copy(k):
        return remote(
            halo_src.at[k], halo_got.at[k], halo_s.at[k], halo_r.at[k], p.z_peer((1, 7)[k], c)
        )

    for d in Z_ORDER:
        resp_copy(0, d).start()
    for d in Z_ORDER:
        table_copy(d).start()
    for d in Z_ORDER:
        resp_copy(1, d).start()
    for h in range(2):
        sib_resp(h).start()
    for k in range(2):
        halo_copy(k).start()

    for q in range(4):
        @pl.when(jnp.logical_not(mine(q)))
        def _():
            occ_in(q).wait_recv()

    own = 4 * y + x
    occ_all[own, c] = jnp.concatenate([occ_got[q] for q in range(4)], axis=0).astype(BF16)
    occ_gather.start()

    def arrange(parts):
        for k in range(8):
            rows32[:, k, :] = parts[k]

    def by_core(mine_part, other_part):
        first = [jnp.where(c == 0, mine_part(r), other_part(r)) for r in range(4)]
        last = [jnp.where(c == 0, other_part(r), mine_part(r)) for r in range(4)]
        return first + last

    def rows_half():
        return rows32[pl.ds((SLAB // 2) * c, SLAB // 2)].reshape(HALF, N).astype(BF16)

    def slab_of(ref):
        def part(r):
            return ref(r // 2).astype(F32)[SLAB * (r % 2) : SLAB * (r % 2) + SLAB]

        return part

    for h in range(2):
        sib_resp(h).wait_recv()
    arrange(by_core(slab_of(lambda h: resp_got[h, z]), slab_of(lambda h: resp_sib[h])))
    resp_all[own, c] = rows_half()

    occ_gather.forward()

    def unpack(h):
        for d in Z_ORDER:
            resp_wait(h, d)
        for r in range(2):
            whole = [
                resp_got[h, s].astype(F32)[SLAB * r : SLAB * r + SLAB] for s in range(NZ)
            ]
            resp_full[2 * h + r] = jnp.concatenate(whole, axis=0).astype(BF16)

    unpack(0)
    for d in Z_ORDER:
        src = lax.rem(z + d, NZ)
        remote(
            table_got.at[src], table_got.at[src], table_s.at[0], table_r.at[src], p.z_peer(d, c)
        ).wait_recv()
    table[...] = table_got[...].reshape(N, N).T

    occ_gather.hand_on(1)
    occ_gather.hand_on(3)

    def pick(t, values):
        out = values[0]
        for i in range(1, 4):
            out = jnp.where(t == i, values[i], out)
        return out

    STEPS_X = ((0, 1, 0, 1), (3, 0, 3, 1), (3, 2, 0, 2), (1, 2, 3, 2))
    STEPS_Y = ((0, 0, 1, 1), (0, 3, 1, 3), (3, 0, 2, 1), (2, 3, 2, 2))

    def slots_of(t):
        out = []
        for q in range(4):
            dx = pick(t, [STEPS_X[i][q] for i in range(4)])
            dy = pick(t, [STEPS_Y[i][q] for i in range(4)])
            out.append(4 * mod4(y + dy) + mod4(x + dx))
        return out

    def pairs(h, t):
        orbitals = [occ_all[sl].reshape(N, N) for sl in slots_of(t)]
        which = [(r, q) for r in range(2) for q in range(4)]
        first = [
            jnp.dot(
                orbitals[q] * resp_full[2 * h + r], ct_ref[...], preferred_element_type=F32
            ).astype(BF16)
            for r, q in which
        ]
        weighted = [
            (jnp.dot(c_ref[...], f, preferred_element_type=F32) * table[...]).astype(BF16)
            for f in first
        ]
        third = [
            jnp.dot(ct_ref[...], w, preferred_element_type=F32).astype(BF16) for w in weighted
        ]
        for r in range(2):
            acc = total[r]
            for q in range(4):
                potential = jnp.dot(third[4 * r + q], c_ref[...], preferred_element_type=F32)
                acc = acc + orbitals[q].astype(F32) * potential
            total[r] = acc

    def rs_copy(h, d):
        to = lax.rem(z + d, NZ)
        return remote(
            rs_src.at[h, to],
            rs_got.at[h, z],
            rs_s.at[7 * h + d - 1],
            rs_r.at[8 * h + z],
            p.z_peer(d, c),
        )

    def reduce_start(h):
        for s in range(NZ):
            pair = [total[r, SLAB * s : SLAB * s + SLAB, :] for r in range(2)]
            rs_src[h, s] = (jnp.concatenate(pair, axis=0) * (1.0 / BANDS)).astype(BF16)
        for d in Z_ORDER:
            rs_copy(h, d).start()
        for r in range(2):
            start = pl.multiple_of(SLAB * z, 8)
            exch_own[2 * h + r] = total[r, pl.ds(start, SLAB), :] * (1.0 / BANDS)

    def reduce_finish(h):
        acc = [exch_own[2 * h + r] for r in range(2)]
        for d in Z_ORDER:
            src = lax.rem(z + d, NZ)
            remote(
                rs_got.at[h, src],
                rs_got.at[h, src],
                rs_s.at[0],
                rs_r.at[8 * h + src],
                p.z_peer(d, c),
            ).wait_recv()
            got = rs_got[h, src].astype(F32)
            for r in range(2):
                acc[r] = acc[r] + got[SLAB * r : SLAB * r + SLAB]
        for r in range(2):
            exch_own[2 * h + r] = acc[r]
        exch_wire[h] = jnp.concatenate(acc, axis=0).astype(BF16)

    total[...] = jnp.zeros_like(total)

    def step_one(t, carry):
        @pl.when(t == 1)
        def _():
            occ_gather.hand_on(2)

        for sl in slots_of(t):
            occ_gather.wait_sib(sl)
        pairs(0, t)
        return carry

    lax.fori_loop(0, 4, step_one, 0)
    reduce_start(0)
    resp_gather.start()
    unpack(1)
    total[...] = jnp.zeros_like(total)

    def step_two(t, carry):
        @pl.when(t == 1)
        def _():
            resp_gather.forward()

        pairs(1, t)
        return carry

    lax.fori_loop(0, 4, step_two, 0)
    reduce_start(1)

    for e in (1, 3, 2):
        resp_gather.hand_on(e)
    for k in range(2):
        remote(
            halo_src.at[k], halo_got.at[k], halo_s.at[k], halo_r.at[k], p.z_peer((7, 1)[k], c)
        ).wait_recv()
    for j in range(8):
        band = resp_ref[j].astype(F32)
        above = jnp.concatenate([halo_got[0, j : j + 1, :], band[: SLAB - 1]], axis=0)
        below = jnp.concatenate([band[1:], halo_got[1, j : j + 1, :]], axis=0)
        left = jnp.concatenate([band[:, N - 1 :], band[:, : N - 1]], axis=1)
        right = jnp.concatenate([band[:, 1:], band[:, :1]], axis=1)
        value = 0.5 * (4.0 * band - ((above + below) + left + right))
        value = value + (local_ref[...] - energy_ref[j]) * band
        weights = [jnp.where(index_ref[j] == k, 1.0, 0.0) for k in range(3)]
        perturb = weights[0] * field_ref[0] + weights[1] * field_ref[1] + weights[2] * field_ref[2]
        res_ref[j] = value + perturb * ground_ref[j].astype(F32)

    row = lax.broadcasted_iota(jnp.int32, (256, BANDS), 0)
    col = lax.broadcasted_iota(jnp.int32, (256, BANDS), 1)
    chip, member = row // 16, row % 8
    chip_x, chip_y = chip % 4, chip // 4
    natural = 32 * chip_x + 16 * (chip_y % 2) + 8 * (member // 4) + 4 * (chip_y // 2) + member % 4
    spread[...] = jnp.where(natural == col, 1.0, 0.0).astype(BF16)
    parity = (lax.broadcasted_iota(jnp.int32, (8, 256), 1) // 8) % 2

    for s in range(16):
        resp_gather.wait_sib(s)

    reduce_finish(0)
    reduce_finish(1)

    def sib_exch(h):
        return remote(exch_wire.at[h], resp_sib.at[2 + h], sib_s.at[2 + h], sib_r.at[2 + h], p.sibling)

    for h in range(2):
        sib_exch(h).start()

    zero = jnp.zeros((SLAB, N), F32)
    own_part = slab_of(lambda h: exch_wire[h])
    arrange(by_core(own_part, lambda r: zero))
    left_rows = rows32[...].reshape(N, N).astype(BF16)
    part = jnp.zeros((16, 256), F32)
    for a in range(SLAB // 2):
        bands = resp_all[:, a // 6, 16 * (a % 6) : 16 * (a % 6) + 16, :].reshape(256, N)
        part = part + lax.dot_general(
            left_rows[16 * a : 16 * a + 16],
            bands,
            (((1,), (1,)), ((), ())),
            preferred_element_type=F32,
        )
    folded = jnp.where(parity == 0, part[:8], part[8:])
    pieces = jnp.concatenate(split_bf16(folded), axis=0).astype(BF16)
    pieces = jnp.dot(pieces, spread[...], preferred_element_type=F32)
    gram_z[2 * z + c] = (pieces[:8] + pieces[8:16] + pieces[16:24]) * (1.0 / (N * N))

    z_line = [(d, k) for d in Z_ORDER for k in (0, 1)] + [(0, 1)]

    def line_core(k):
        return (1 - k) * c + k * (1 - c)

    def gram_copy(i):
        d, k = z_line[i]
        mine_slot = gram_z.at[2 * z + c]
        return remote(
            mine_slot, mine_slot, gz_s.at[i], gz_r.at[2 * z + c], p.z_peer(d, line_core(k))
        )

    for i in range(len(z_line)):
        gram_copy(i).start()

    for h in range(2):
        sib_exch(h).wait_recv()
    arrange(by_core(own_part, slab_of(lambda h: resp_sib[2 + h])))
    exch_all[own, c] = rows_half()
    exch_gather.start()

    for d, k in z_line:
        src = 2 * lax.rem(z + d, NZ) + line_core(k)
        slot = gram_z.at[src]
        remote(slot, slot, gz_s.at[0], gz_r.at[src], p.z_peer(d, line_core(k))).wait_recv()
    summed = gram_z[0]
    for i in range(1, 2 * NZ):
        summed = summed + gram_z[i]
    gram_xy[y, x] = summed

    def gx_copy(d):
        slot = gram_xy.at[y, x]
        return remote(slot, slot, gx_s.at[d - 1], gx_r.at[x], p.dev(mod4(x + d), y, z, c))

    def gy_copy(d):
        slot = gram_xy.at[y]
        return remote(slot, slot, gy_s.at[d - 1], gy_r.at[y], p.dev(x, mod4(y + d), z, c))

    for d in (1, 3, 2):
        gx_copy(d).start()
    exch_gather.forward()
    for d in (1, 3, 2):
        src = mod4(x + d)
        slot = gram_xy.at[y, src]
        remote(slot, slot, gx_s.at[0], gx_r.at[src], p.dev(src, y, z, c)).wait_recv()
    for d in (1, 3, 2):
        gy_copy(d).start()
    for e in (1, 3, 2):
        exch_gather.hand_on(e)
    for d in (1, 3, 2):
        src = mod4(y + d)
        slot = gram_xy.at[src]
        remote(slot, slot, gy_s.at[0], gy_r.at[src], p.dev(x, src, z, c)).wait_recv()

    for i in range(32):
        n_x, n_lo, n_c, n_g = i // 8, (i // 4) % 2, (i // 2) % 2, i % 2
        gram_full[4 * i : 4 * i + 4, :] = gram_xy[2 * n_g + n_lo, n_x, 4 * n_c : 4 * n_c + 4, :]
    gram = gram_full[...]
    gram_full[...] = inverse_factor(0.5 * (gram + gram.T))
    inverse = gram_full[pl.ds(pl.multiple_of(8 * p.b, 8), 8), :]

    for s in range(16):
        exch_gather.wait_sib(s)

    for half in range(2):
        slot = 4 * (2 * half + p.y_lo) + x
        rows32[...] = exch_all[slot].reshape(SLAB, 8, N).astype(F32)
        for r in range(4):
            value = jnp.where(c == 0, rows32[:, r, :], rows32[:, 4 + r, :])
            res_ref[4 * half + r] = res_ref[4 * half + r] - EXCHANGE_FRACTION * value

    pieces = jnp.concatenate(split_bf16(inverse), axis=0).astype(BF16)
    wide = lax.dot_general(
        pieces, spread[...], (((1,), (1,)), ((), ())), preferred_element_type=F32
    )
    parity = jnp.concatenate([parity] * 3, axis=0)
    left = jnp.concatenate(
        [jnp.where(parity == 0, wide, 0.0), jnp.where(parity == 1, wide, 0.0)], axis=0
    ).astype(BF16)
    for a in range(SLAB // 2):
        vectors = exch_all[:, a // 6, 16 * (a % 6) : 16 * (a % 6) + 16, :].reshape(256, N)
        out = jnp.dot(left, vectors, preferred_element_type=F32)
        for k in range(2):
            o = out[24 * k : 24 * k + 24]
            proj32[:, 2 * a + k, :] = (o[16:24] + o[8:16]) + o[:8]
    for j in range(8):
        proj_ref[j] = proj32[j].astype(BF16)

    for r in range(4):
        @pl.when(jnp.logical_not(mine(r)))
        def _():
            occ_out(r).wait_send()

    for d in range(1, NZ):
        table_copy(d).wait_send()
        for h in range(2):
            resp_copy(h, d).wait_send()
            rs_copy(h, d).wait_send()
    for h in range(2):
        sib_resp(h).wait_send()
        sib_exch(h).wait_send()
        halo_copy(h).wait_send()
    for i in range(len(z_line)):
        gram_copy(i).wait_send()
    for d in (1, 2, 3):
        gx_copy(d).wait_send()
        gy_copy(d).wait_send()
    for gather in (occ_gather, resp_gather, exch_gather):
        gather.finish()


def on_device(*arguments):
    table = cosine_table(N)
    vmem = pl.BlockSpec(memory_space=pltpu.VMEM)
    smem = pl.BlockSpec(memory_space=pltpu.SMEM)
    dma = lambda n: pltpu.SemaphoreType.DMA((n,))
    scratch = [
        pltpu.VMEM((4, SLAB, N), F32),
        pltpu.VMEM((4, SLAB, N), F32),
        pltpu.VMEM((2, NZ, 2 * SLAB, N), BF16),
        pltpu.VMEM((4, 2 * SLAB, N), BF16),
        pltpu.VMEM((4, N, N), BF16),
        pltpu.VMEM((NZ, SLAB, N), F32),
        pltpu.VMEM((N, N), F32),
        pltpu.VMEM((2, 8, N), F32),
        pltpu.VMEM((2, 8, N), F32),
        pltpu.VMEM((16, 2, HALF, N), BF16),
        pltpu.VMEM((16, 2, HALF, N), BF16),
        pltpu.VMEM((16, 2, HALF, N), BF16),
        pltpu.VMEM((2, N, N), F32),
        pltpu.VMEM((2, NZ, 2 * SLAB, N), BF16),
        pltpu.VMEM((2, NZ, 2 * SLAB, N), BF16),
        pltpu.VMEM((SLAB, 8, N), F32),
        pltpu.VMEM((4, SLAB, N), F32),
        pltpu.VMEM((2, 2 * SLAB, N), BF16),
        pltpu.VMEM((2 * NZ, 8, BANDS), F32),
        pltpu.VMEM((4, 4, 8, BANDS), F32),
        pltpu.VMEM((BANDS, BANDS), F32),
        pltpu.VMEM((256, BANDS), BF16),
        pltpu.VMEM((8, SLAB, N), F32),
    ]
    counts = [4, 4, 14, 16, 4, 4, 7, 8, 2, 2, 14, 16, 15, 16, 3, 4, 3, 4] + [3, 12, 16, 16, 16] * 3
    scratch += [dma(n) for n in counts]
    return pl.pallas_call(
        kernel,
        out_shape=(
            jax.ShapeDtypeStruct((8, SLAB, N), BF16),
            jax.ShapeDtypeStruct((8, SLAB, N), F32),
        ),
        in_specs=[vmem, vmem, vmem, smem, smem, vmem, vmem, vmem, vmem, vmem],
        out_specs=(vmem, vmem),
        scratch_shapes=scratch,
        compiler_params=pltpu.CompilerParams(
            collective_id=0, has_side_effects=True, vmem_limit_bytes=48 << 20
        ),
        cost_estimate=pl.CostEstimate(
            flops=4 * 64 * 2 * N**3, bytes_accessed=4 << 20, transcendentals=0
        ),
    )(*arguments, jnp.asarray(table), jnp.asarray(np.ascontiguousarray(table.T)))


def solution(mesh):
    return jax.shard_map(
        on_device,
        mesh=mesh,
        in_specs=(
            P(("grp", "band"), "ga", None),
            P("band", "ga", None),
            P("band", "ga", None),
            P("band"),
            P("band"),
            P("ga", None),
            P(None, "ga", None),
            P(None, "ga"),
        ),
        out_specs=(P("band", "ga", None), P("band", "ga", None)),
        check_vma=False,
    )
```

```python
import functools

import jax
import jax.numpy as jnp
import ml_dtypes
import numpy as np
from jax import lax
from jax.experimental import pallas as pl
from jax.experimental.pallas import tpu as pltpu
from jax.sharding import PartitionSpec as P

EXCHANGE_FRACTION = 0.25
F32, BF16 = jnp.float32, jnp.bfloat16
MESH = pl.DeviceIdType.MESH
N = 192
NZ = 8
SLAB = N // NZ
HALF = N // 2
BANDS = 128


def cosine_table(length):
    rows = np.arange(length, dtype=np.float32)[:, None]
    cols = np.arange(length, dtype=np.float32)[None]
    one, two = np.sqrt(np.float32(1.0 / length)), np.sqrt(np.float32(2.0 / length))
    factor = np.where(rows == 0, one, two).astype(np.float32)
    angle = np.float32(np.pi) * (cols + np.float32(0.5)) * rows / np.float32(length)
    return (factor * np.cos(angle)).astype(ml_dtypes.bfloat16)


def pack_one(slab):
    ends = slab[:, 128:]
    ends = jnp.concatenate(
        [
            jnp.concatenate([ends[:8], ends[8:16]], axis=1),
            jnp.concatenate([ends[16:], jnp.zeros((8, 64), F32)], axis=1),
        ],
        axis=0,
    )
    unused = jnp.zeros((WIRE_ONE - SLAB - 16, 128), F32)
    return jnp.concatenate([slab[:, :128], ends, unused], axis=0).astype(BF16)


def unpack_one(wire):
    value = wire.astype(F32)
    ends = value[SLAB : SLAB + 16]
    ends = jnp.concatenate([ends[:8, :64], ends[:8, 64:], ends[8:, :64]], axis=0)
    return [jnp.concatenate([value[:SLAB], ends], axis=1)]


def tree_sum(terms):
    while len(terms) > 1:
        terms = [a + b for a, b in zip(terms[::2], terms[1::2])] + terms[len(terms) & ~1 :]
    return terms[0]


def inverse_factor(gram, halfway):
    lane = lax.broadcasted_iota(jnp.int32, (8, BANDS), 1)
    sub = lax.broadcasted_iota(jnp.int32, (8, BANDS), 0)
    count = BANDS // 8
    blocks = [gram[8 * i : 8 * i + 8, :] for i in range(count)]
    done = []
    for b in range(count):
        if b == 9:
            halfway()
        k0 = 8 * b
        inside = (lane >= k0) & (lane < k0 + 8)
        rows = [jnp.broadcast_to(blocks[b][t : t + 1, :], (8, BANDS)) for t in range(8)]
        a = [
            [jnp.broadcast_to(rows[t][:, k0 + s : k0 + s + 1], (8, BANDS)) for s in range(t + 1)]
            for t in range(8)
        ]
        low = [[None] * 8 for _ in range(8)]
        rinv = [None] * 8
        for t in range(8):
            rinv[t] = lax.rsqrt(a[t][t])
            for u in range(t + 1, 8):
                low[u][t] = a[u][t] * rinv[t]
            for u in range(t + 1, 8):
                for s in range(t + 1, u + 1):
                    a[u][s] = a[u][s] - low[u][t] * low[s][t]
        inv = [[None] * 8 for _ in range(8)]
        for s in range(8):
            inv[s][s] = rinv[s]
            for t in range(s + 1, 8):
                acc = tree_sum([low[t][u] * inv[u][s] for u in range(s, t)])
                inv[t][s] = -(acc * rinv[t])
        unit = [
            jnp.where(lane == k0 + t, 1.0, jnp.where(inside, 0.0, rows[t])) for t in range(8)
        ]
        panel = [tree_sum([inv[t][s] * unit[s] for s in range(t + 1)]) for t in range(8)]
        packed = panel[0]
        for t in range(1, 8):
            packed = jnp.where(sub == t, panel[t], packed)
        done.append(jnp.where(lane <= sub + k0, packed, 0.0))
        for i in range(b + 1, count):
            column = [
                jnp.broadcast_to(blocks[i][:, k0 + s : k0 + s + 1], (8, BANDS)) for s in range(8)
            ]
            new = jnp.where(inside, 0.0, blocks[i])
            factor = [tree_sum([inv[t][s] * column[s] for s in range(t + 1)]) for t in range(8)]
            blocks[i] = new - tree_sum([factor[t] * panel[t] for t in range(8)])
    return jnp.concatenate(done, axis=0)


def split_bf16(value):
    first = value.astype(BF16)
    rest = value - first.astype(F32)
    second = rest.astype(BF16)
    third = (rest - second.astype(F32)).astype(BF16)
    return [first.astype(F32), second.astype(F32), third.astype(F32)]


def mod4(i):
    return lax.rem(i, 4)


class PlaneGather:
    def __init__(self, place, ref, first, second, sib, got, got_sib):
        self.place, self.ref = place, ref
        self.s_first, self.s_second, self.s_sib = first, second, sib
        self.r_ici, self.r_sib = got, got_sib

    def slot(self, d, e):
        p = self.place
        f, s = mod4(p.f + d), mod4(p.s + e)
        return (1 - p.c) * (4 * s + f) + p.c * (4 * f + s)

    def peer(self, d, e):
        p = self.place
        f, s = mod4(p.f + d), mod4(p.s + e)
        return p.dev((1 - p.c) * f + p.c * s, (1 - p.c) * s + p.c * f, p.z, p.c)

    def copy(self, sl, half, send, recv, device):
        part = self.ref.at[sl, half]
        return pltpu.make_async_remote_copy(
            src_ref=part,
            dst_ref=part,
            send_sem=send,
            recv_sem=recv,
            device_id=device,
            device_id_type=MESH,
        )

    def first_copy(self, d):
        sl = self.slot(0, 0)
        return self.copy(sl, self.place.c, self.s_first.at[d - 1], self.r_ici.at[sl], self.peer(d, 0))

    def second_copy(self, d, e):
        sl = self.slot(d, 0)
        return self.copy(
            sl, self.place.c, self.s_second.at[3 * d + e - 1], self.r_ici.at[sl], self.peer(0, e)
        )

    def sib_copy(self, d, e):
        p = self.place
        sl = self.slot(d, e)
        return self.copy(sl, p.c, self.s_sib.at[4 * d + e], self.r_sib.at[sl], p.sibling)

    def start(self):
        for d in (1, 3, 2):
            self.first_copy(d).start()
        for e in (1, 3, 2):
            self.second_copy(0, e).start()
        self.sib_copy(0, 0).start()

    def forward(self):
        for d in (1, 3, 2):
            sl = self.slot(d, 0)
            self.copy(
                sl, self.place.c, self.s_first.at[0], self.r_ici.at[sl], self.peer(d, 0)
            ).wait_recv()
            for e in (1, 3, 2):
                self.second_copy(d, e).start()
            self.sib_copy(d, 0).start()

    def hand_on(self, offsets):
        for d, e in offsets:
            sl = self.slot(d, e)
            self.copy(
                sl, self.place.c, self.s_first.at[0], self.r_ici.at[sl], self.peer(0, e)
            ).wait_recv()
            self.sib_copy(d, e).start()

    def wait_sib(self, sl):
        p = self.place
        self.copy(sl, 1 - p.c, self.s_sib.at[0], self.r_sib.at[sl], p.sibling).wait_recv()

    def finish(self):
        for d in (1, 2, 3):
            self.first_copy(d).wait_send()
        for d in range(4):
            for e in (1, 2, 3):
                self.second_copy(d, e).wait_send()
        for d in range(4):
            for e in range(4):
                self.sib_copy(d, e).wait_send()


class Place:
    def __init__(self):
        self.g = lax.axis_index("grp")
        self.b = lax.axis_index("band")
        self.z = lax.axis_index("ga")
        self.x = lax.div(self.b, 4)
        self.y_lo = lax.rem(lax.div(self.b, 2), 2)
        self.c = lax.rem(self.b, 2)
        self.y = 2 * self.g + self.y_lo
        self.f = (1 - self.c) * self.x + self.c * self.y
        self.s = (1 - self.c) * self.y + self.c * self.x
        self.sibling = self.dev(self.x, self.y, self.z, 1 - self.c)

    def dev(self, x, y, z, c):
        return {"grp": lax.div(y, 2), "band": 4 * x + 2 * lax.rem(y, 2) + c, "ga": z}

    def z_peer(self, d, c):
        return self.dev(self.x, self.y, lax.rem(self.z + d, NZ), c)


def remote(src, dst, send, recv, device):
    return pltpu.make_async_remote_copy(
        src_ref=src,
        dst_ref=dst,
        send_sem=send,
        recv_sem=recv,
        device_id=device,
        device_id_type=MESH,
    )


Z_ORDER = (4, 3, 5, 2, 6, 1, 7)
NEAR = ((0, 1), (0, 3), (0, 2))
LATE = ((1, 1), (1, 3), (3, 1), (3, 3), (1, 2), (2, 1), (3, 2), (2, 3), (2, 2))
WIRE_ONE = 48
WIRE = 80


def pack(pair):
    ends = jnp.concatenate([pair[:SLAB, 128:], pair[SLAB:, 128:]], axis=1)
    unused = jnp.zeros((WIRE - 3 * SLAB, 128), F32)
    return jnp.concatenate([pair[:, :128], ends, unused], axis=0).astype(BF16)


def unpack(wire):
    value = wire.astype(F32)
    ends = value[2 * SLAB : 3 * SLAB]
    return [
        jnp.concatenate([value[:SLAB], ends[:, :64]], axis=1),
        jnp.concatenate([value[SLAB : 2 * SLAB], ends[:, 64:]], axis=1),
    ]


def kernel(
    occ_hbm,
    resp_hbm,
    ground_hbm,
    index_hbm,
    energy_hbm,
    local_hbm,
    field_hbm,
    table_hbm,
    c_hbm,
    ct_hbm,
    proj_ref,
    res_ref,
    occ_ref,
    resp_ref,
    ground_ref,
    index_ref,
    energy_ref,
    local_ref,
    field_ref,
    c_ref,
    ct_ref,
    occ_src,
    occ_got,
    resp_got,
    resp_sib,
    resp_full,
    table_got,
    table,
    halo_src,
    halo_got,
    occ_all,
    resp_all,
    exch_all,
    total,
    rs_src,
    rs_got,
    rs_src_one,
    rs_got_one,
    rows32,
    exch_own,
    exch_wire,
    gram_z,
    gram_xy,
    gram_full,
    spread,
    proj32,
    *sems,
):
    p = Place()
    z, c, x, y, g = p.z, p.c, p.x, p.y, p.g
    sems = list(sems)
    take = lambda: sems.pop(0)
    in_s = take()
    occ_s, occ_r = take(), take()
    resp_s, resp_r = take(), take()
    sib_s, sib_r = take(), take()
    table_s, table_r = take(), take()
    table_sib_s, table_sib_r = take(), take()
    halo_s, halo_r = take(), take()
    rs_s, rs_r = take(), take()
    gz_s, gz_r = take(), take()
    gp_s, gp_r = take(), take()
    occ_gather = PlaneGather(p, occ_all, *[take() for _ in range(5)])
    resp_gather = PlaneGather(p, resp_all, *[take() for _ in range(5)])
    exch_gather = PlaneGather(p, exch_all, *[take() for _ in range(5)])

    loads = [
        pltpu.make_async_copy(src, dst, in_s.at[i])
        for i, (src, dst) in enumerate(
            (
                (occ_hbm, occ_ref),
                (resp_hbm, resp_ref),
                (table_hbm, table_got.at[z]),
                (c_hbm, c_ref),
                (ct_hbm, ct_ref),
                (ground_hbm, ground_ref),
                (field_hbm, field_ref),
                (local_hbm, local_ref),
                (index_hbm, index_ref),
                (energy_hbm, energy_ref),
            )
        )
    ]
    for load in loads:
        load.start()

    barrier = pltpu.get_barrier_semaphore()
    peers = [p.z_peer(d, k) for d in range(1, NZ) for k in (0, 1)]
    peers += [p.sibling]
    plane = [(d, e) for d in (2, 1, 3, 0) for e in (2, 1, 3, 0) if (d, e) != (0, 0)]
    peers += [p.dev(mod4(x + d), mod4(y + e), z, c) for d, e in plane]
    for peer in peers:
        pl.semaphore_signal(barrier, inc=1, device_id=peer, device_id_type=MESH)

    for load in loads[:3]:
        load.wait()
    for r in range(4):
        occ_src[r] = pack_one(occ_ref[r].astype(F32))
    for h in range(2):
        pair = [resp_ref[4 * g + 2 * h + r].astype(F32) for r in range(2)]
        resp_got[h, z] = pack(jnp.concatenate(pair, axis=0))
    edge = [resp_ref[j].astype(F32) for j in range(8)]
    halo_src[0] = jnp.concatenate([e[SLAB - 1 : SLAB] for e in edge], axis=0)
    halo_src[1] = jnp.concatenate([e[0:1] for e in edge], axis=0)
    pl.semaphore_wait(barrier, len(peers))

    half_of_z = lax.div(z, 4)
    quarter = lax.rem(z, 4)

    def occ_out(r):
        return remote(
            occ_src.at[r],
            occ_got.at[quarter],
            occ_s.at[r],
            occ_r.at[quarter],
            p.dev(x, y, 4 * c + r, half_of_z),
        )

    def occ_in(q):
        return remote(
            occ_src.at[q],
            occ_got.at[q],
            occ_s.at[q],
            occ_r.at[q],
            p.dev(x, y, 4 * c + q, half_of_z),
        )

    def mine(r):
        return (half_of_z == c) & (quarter == r)

    for r in range(4):
        @pl.when(jnp.logical_not(mine(r)))
        def _():
            occ_out(r).start()

        @pl.when(mine(r))
        def _():
            occ_got[r] = occ_src[r]

    def table_copy(i):
        d = 2 * i + 2 - c
        return remote(
            table_got.at[z], table_got.at[z], table_s.at[i], table_r.at[z], p.z_peer(d, c)
        )

    def table_on(i):
        src = lax.rem(z + NZ - (2 * i + 2 - c), NZ)
        slot = table_got.at[src]
        return remote(slot, slot, table_sib_s.at[i], table_sib_r.at[src], p.sibling)

    def table_wait(i):
        src = lax.rem(z + NZ - (2 * i + 2 - c), NZ)
        slot = table_got.at[src]
        remote(slot, slot, table_s.at[0], table_r.at[src], p.sibling).wait_recv()
        table_on(i).start()

    def table_wait_sib(i):
        src = lax.rem(z + NZ - (2 * i + 1 + c), NZ)
        slot = table_got.at[src]
        remote(slot, slot, table_sib_s.at[0], table_sib_r.at[src], p.sibling).wait_recv()

    def for_table(core, act):
        for i in range(3):
            act(i)

        @pl.when(core == 1)
        def _():
            act(3)

    def resp_copy(h, d):
        return remote(
            resp_got.at[h, z],
            resp_got.at[h, z],
            resp_s.at[7 * h + d - 1],
            resp_r.at[8 * h + z],
            p.z_peer(d, c),
        )

    def resp_wait(h, d):
        src = lax.rem(z + d, NZ)
        remote(
            resp_got.at[h, src],
            resp_got.at[h, src],
            resp_s.at[0],
            resp_r.at[8 * h + src],
            p.z_peer(d, c),
        ).wait_recv()

    def sib_resp(h):
        return remote(resp_got.at[h, z], resp_sib.at[h], sib_s.at[h], sib_r.at[h], p.sibling)

    def halo_copy(k):
        return remote(
            halo_src.at[k], halo_got.at[k], halo_s.at[k], halo_r.at[k], p.z_peer((1, 7)[k], c)
        )

    for_table(c, lambda i: table_copy(i).start())
    for d in Z_ORDER:
        resp_copy(0, d).start()
    for d in Z_ORDER:
        resp_copy(1, d).start()
    for h in range(2):
        sib_resp(h).start()
    for k in range(2):
        halo_copy(k).start()

    for q in range(4):
        @pl.when(jnp.logical_not(mine(q)))
        def _():
            occ_in(q).wait_recv()

    own = 4 * y + x
    occ_all[own, c] = jnp.concatenate(
        [unpack_one(occ_got[q])[0] for q in range(4)], axis=0
    ).astype(BF16)
    occ_gather.start()

    def arrange(parts):
        for k in range(8):
            rows32[:, k, :] = parts[k]

    def by_core(mine_part, other_part):
        first = [jnp.where(c == 0, mine_part(r), other_part(r)) for r in range(4)]
        last = [jnp.where(c == 0, other_part(r), mine_part(r)) for r in range(4)]
        return first + last

    def rows_half():
        return rows32[pl.ds((SLAB // 2) * c, SLAB // 2)].reshape(HALF, N).astype(BF16)

    def slab_of(ref):
        def part(r):
            return unpack(ref(r // 2))[r % 2]

        return part

    for h in range(2):
        sib_resp(h).wait_recv()
    arrange(by_core(slab_of(lambda h: resp_got[h, z]), slab_of(lambda h: resp_sib[h])))
    resp_all[own, c] = rows_half()

    for load in loads[3:]:
        load.wait()
    for_table(c, table_wait)
    occ_gather.forward()
    occ_gather.hand_on(NEAR)
    for_table(1 - c, table_wait_sib)
    table[...] = table_got[...].reshape(N, N).T

    def whole_bands(h):
        for d in Z_ORDER:
            resp_wait(h, d)
        parts = [unpack(resp_got[h, s]) for s in range(NZ)]
        for r in range(2):
            whole = [parts[s][r] for s in range(NZ)]
            resp_full[2 * h + r] = jnp.concatenate(whole, axis=0).astype(BF16)

    whole_bands(0)

    def pick(t, values):
        out = values[0]
        for i in range(1, 4):
            out = jnp.where(t == i, values[i], out)
        return out

    STEPS_X = ((0, 1, 0, 3), (0, 2, 0, 1), (1, 3, 3, 1), (2, 3, 2, 2))
    STEPS_Y = ((0, 0, 1, 0), (3, 0, 2, 1), (3, 1, 3, 2), (1, 2, 3, 2))

    def slots_of(t):
        out = []
        for q in range(4):
            dx = pick(t, [STEPS_X[i][q] for i in range(4)])
            dy = pick(t, [STEPS_Y[i][q] for i in range(4)])
            out.append(4 * mod4(y + dy) + mod4(x + dx))
        return out

    def pairs(slots, bands):
        orbitals = [occ_all[sl].reshape(N, N) for sl in slots]
        which = [(r, q) for r in bands for q in range(len(slots))]
        first = [
            jnp.dot(orbitals[q] * resp_full[r], ct_ref[...], preferred_element_type=F32).astype(BF16)
            for r, q in which
        ]
        weighted = [
            (jnp.dot(c_ref[...], f, preferred_element_type=F32) * table[...]).astype(BF16)
            for f in first
        ]
        third = [
            jnp.dot(ct_ref[...], w, preferred_element_type=F32).astype(BF16) for w in weighted
        ]
        for r in bands:
            acc = total[r]
            for i, (band, q) in enumerate(which):
                if band == r:
                    potential = jnp.dot(third[i], c_ref[...], preferred_element_type=F32)
                    acc = acc + orbitals[q].astype(F32) * potential
            total[r] = acc

    groups = ((0, 1), (2,), (3,))

    def rs_refs(h):
        if h == 0:
            return rs_src, rs_got
        return rs_src_one.at[h - 1], rs_got_one.at[h - 1]

    def rs_copy(h, d):
        to = lax.rem(z + d, NZ)
        src, dst = rs_refs(h)
        return remote(
            src.at[to], dst.at[z], rs_s.at[7 * h + d - 1], rs_r.at[8 * h + z], p.z_peer(d, c)
        )

    def reduce_start(h):
        src, _ = rs_refs(h)
        for s in range(NZ):
            out = [total[r, SLAB * s : SLAB * s + SLAB, :] * (1.0 / BANDS) for r in groups[h]]
            src[s] = pack(jnp.concatenate(out, axis=0)) if h == 0 else pack_one(out[0])
        for d in Z_ORDER:
            rs_copy(h, d).start()
        start = pl.multiple_of(SLAB * z, 8)
        for r in groups[h]:
            exch_own[r] = total[r, pl.ds(start, SLAB), :] * (1.0 / BANDS)

    def reduce_finish(h):
        _, dst = rs_refs(h)
        acc = [exch_own[r] for r in groups[h]]
        for d in Z_ORDER:
            src = lax.rem(z + d, NZ)
            slot = dst.at[src]
            remote(slot, slot, rs_s.at[0], rs_r.at[8 * h + src], p.z_peer(d, c)).wait_recv()
            got = unpack(dst[src]) if h == 0 else unpack_one(dst[src])
            acc = [a + b for a, b in zip(acc, got)]
        for r, a in zip(groups[h], acc):
            exch_own[r] = a

    total[...] = jnp.zeros_like(total)

    def step_one(t, carry):
        @pl.when(t == 3)
        def _():
            resp_gather.start()

        for sl in slots_of(t):
            occ_gather.wait_sib(sl)
        pairs(slots_of(t), groups[0])

        @pl.when(t == 0)
        def _():
            occ_gather.hand_on(LATE[:4])

        @pl.when(t == 1)
        def _():
            occ_gather.hand_on(LATE[4:])

        return carry

    lax.fori_loop(0, 4, step_one, 0)
    reduce_start(0)
    whole_bands(1)

    def later_step(bands):
        def step(t, carry):
            pairs([8 * t + q for q in range(8)], bands)
            return carry

        return step

    lax.fori_loop(0, 2, later_step(groups[1]), 0)
    reduce_start(1)
    resp_gather.forward()
    resp_gather.hand_on(NEAR)
    lax.fori_loop(0, 2, later_step(groups[2]), 0)
    reduce_start(2)

    resp_gather.hand_on(LATE)
    for k in range(2):
        remote(
            halo_src.at[k], halo_got.at[k], halo_s.at[k], halo_r.at[k], p.z_peer((7, 1)[k], c)
        ).wait_recv()
    for j in range(8):
        band = resp_ref[j].astype(F32)
        above = jnp.concatenate([halo_got[0, j : j + 1, :], band[: SLAB - 1]], axis=0)
        below = jnp.concatenate([band[1:], halo_got[1, j : j + 1, :]], axis=0)
        left = jnp.concatenate([band[:, N - 1 :], band[:, : N - 1]], axis=1)
        right = jnp.concatenate([band[:, 1:], band[:, :1]], axis=1)
        value = 0.5 * (4.0 * band - ((above + below) + left + right))
        value = value + (local_ref[...] - energy_ref[j]) * band
        weights = [jnp.where(index_ref[j] == k, 1.0, 0.0) for k in range(3)]
        perturb = weights[0] * field_ref[0] + weights[1] * field_ref[1] + weights[2] * field_ref[2]
        res_ref[j] = value + perturb * ground_ref[j].astype(F32)

    row = lax.broadcasted_iota(jnp.int32, (256, BANDS), 0)
    col = lax.broadcasted_iota(jnp.int32, (256, BANDS), 1)
    chip, member = row // 16, row % 8
    chip_x, chip_y = chip % 4, chip // 4
    natural = 32 * chip_x + 16 * (chip_y % 2) + 8 * (member // 4) + 4 * (chip_y // 2) + member % 4
    spread[...] = jnp.where(natural == col, 1.0, 0.0).astype(BF16)
    parity = (lax.broadcasted_iota(jnp.int32, (8, 256), 1) // 8) % 2

    for s in range(16):
        resp_gather.wait_sib(s)

    def sib_exch(h):
        return remote(exch_wire.at[h], resp_sib.at[2 + h], sib_s.at[2 + h], sib_r.at[2 + h], p.sibling)

    def sib_exch_start(h):
        exch_wire[h] = pack(jnp.concatenate([exch_own[2 * h], exch_own[2 * h + 1]], axis=0))
        sib_exch(h).start()

    reduce_finish(0)
    sib_exch_start(0)
    reduce_finish(1)
    reduce_finish(2)
    sib_exch_start(1)

    zero = jnp.zeros((SLAB, N), F32)
    own_part = slab_of(lambda h: exch_wire[h])
    arrange(by_core(own_part, lambda r: zero))
    left_rows = rows32[...].reshape(N, N).astype(BF16)
    part = jnp.zeros((16, 256), F32)
    for a in range(SLAB // 2):
        bands = resp_all[:, a // 6, 16 * (a % 6) : 16 * (a % 6) + 16, :].reshape(256, N)
        part = part + lax.dot_general(
            left_rows[16 * a : 16 * a + 16],
            bands,
            (((1,), (1,)), ((), ())),
            preferred_element_type=F32,
        )
    folded = jnp.where(parity == 0, part[:8], part[8:])
    pieces = jnp.concatenate(split_bf16(folded), axis=0).astype(BF16)
    pieces = jnp.dot(pieces, spread[...], preferred_element_type=F32)
    gram_z[2 * z + c] = (pieces[:8] + pieces[8:16] + pieces[16:24]) * (1.0 / (N * N))

    z_line = [(d, k) for d in Z_ORDER for k in (0, 1)] + [(0, 1)]

    def line_core(k):
        return (1 - k) * c + k * (1 - c)

    def gram_copy(i):
        d, k = z_line[i]
        mine_slot = gram_z.at[2 * z + c]
        return remote(
            mine_slot, mine_slot, gz_s.at[i], gz_r.at[2 * z + c], p.z_peer(d, line_core(k))
        )

    for i in range(len(z_line)):
        gram_copy(i).start()

    for h in range(2):
        sib_exch(h).wait_recv()
    arrange(by_core(own_part, slab_of(lambda h: resp_sib[2 + h])))
    exch_all[own, c] = rows_half()
    exch_gather.start()

    for d, k in z_line:
        src = 2 * lax.rem(z + d, NZ) + line_core(k)
        slot = gram_z.at[src]
        remote(slot, slot, gz_s.at[0], gz_r.at[src], p.z_peer(d, line_core(k))).wait_recv()
    summed = gram_z[0]
    for i in range(1, 2 * NZ):
        summed = summed + gram_z[i]
    gram_xy[y, x] = summed

    def gram_plane(i):
        d, e = plane[i]
        slot = gram_xy.at[y, x]
        device = p.dev(mod4(x + d), mod4(y + e), z, c)
        return remote(slot, slot, gp_s.at[i], gp_r.at[own], device)

    for i in range(len(plane)):
        gram_plane(i).start()
    exch_gather.forward()
    exch_gather.hand_on(NEAR)
    for d, e in plane:
        src_x, src_y = mod4(x + d), mod4(y + e)
        slot = gram_xy.at[src_y, src_x]
        remote(
            slot, slot, gp_s.at[0], gp_r.at[4 * src_y + src_x], p.dev(src_x, src_y, z, c)
        ).wait_recv()

    for i in range(32):
        n_x, n_lo, n_c, n_g = i // 8, (i // 4) % 2, (i // 2) % 2, i % 2
        gram_full[4 * i : 4 * i + 4, :] = gram_xy[2 * n_g + n_lo, n_x, 4 * n_c : 4 * n_c + 4, :]
    gram = gram_full[...]
    gram_full[...] = inverse_factor(
        0.5 * (gram + gram.T), lambda: exch_gather.hand_on(LATE)
    )
    inverse = gram_full[pl.ds(pl.multiple_of(8 * p.b, 8), 8), :]

    for s in range(16):
        exch_gather.wait_sib(s)

    for half in range(2):
        slot = 4 * (2 * half + p.y_lo) + x
        rows32[...] = exch_all[slot].reshape(SLAB, 8, N).astype(F32)
        for r in range(4):
            value = jnp.where(c == 0, rows32[:, r, :], rows32[:, 4 + r, :])
            res_ref[4 * half + r] = res_ref[4 * half + r] - EXCHANGE_FRACTION * value

    pieces = jnp.concatenate(split_bf16(inverse), axis=0).astype(BF16)
    wide = lax.dot_general(
        pieces, spread[...], (((1,), (1,)), ((), ())), preferred_element_type=F32
    )
    parity = jnp.concatenate([parity] * 3, axis=0)
    left = jnp.concatenate(
        [jnp.where(parity == 0, wide, 0.0), jnp.where(parity == 1, wide, 0.0)], axis=0
    ).astype(BF16)
    for a in range(SLAB // 2):
        vectors = exch_all[:, a // 6, 16 * (a % 6) : 16 * (a % 6) + 16, :].reshape(256, N)
        out = jnp.dot(left, vectors, preferred_element_type=F32)
        for k in range(2):
            o = out[24 * k : 24 * k + 24]
            proj32[:, 2 * a + k, :] = (o[16:24] + o[8:16]) + o[:8]
    for j in range(8):
        proj_ref[j] = proj32[j].astype(BF16)

    for r in range(4):
        @pl.when(jnp.logical_not(mine(r)))
        def _():
            occ_out(r).wait_send()

    for_table(c, lambda i: table_copy(i).wait_send())
    for_table(c, lambda i: table_on(i).wait_send())
    for d in range(1, NZ):
        for h in range(2):
            resp_copy(h, d).wait_send()
        for h in range(3):
            rs_copy(h, d).wait_send()
    for h in range(2):
        sib_resp(h).wait_send()
        sib_exch(h).wait_send()
        halo_copy(h).wait_send()
    for i in range(len(z_line)):
        gram_copy(i).wait_send()
    for i in range(len(plane)):
        gram_plane(i).wait_send()
    for gather in (occ_gather, resp_gather, exch_gather):
        gather.finish()


def on_device(*arguments):
    arguments = arguments[:7] + (arguments[7].T,)
    table = cosine_table(N)
    vmem = pl.BlockSpec(memory_space=pltpu.VMEM)
    hbm = pl.BlockSpec(memory_space=pltpu.HBM)
    dma = lambda n: pltpu.SemaphoreType.DMA((n,))
    scratch = [
        pltpu.VMEM((4, SLAB, N), BF16),
        pltpu.VMEM((8, SLAB, N), BF16),
        pltpu.VMEM((8, SLAB, N), BF16),
        pltpu.SMEM((8,), jnp.int32),
        pltpu.SMEM((8,), F32),
        pltpu.VMEM((SLAB, N), F32),
        pltpu.VMEM((3, SLAB, N), F32),
        pltpu.VMEM((N, N), BF16),
        pltpu.VMEM((N, N), BF16),
        pltpu.VMEM((4, WIRE_ONE, 128), BF16),
        pltpu.VMEM((4, WIRE_ONE, 128), BF16),
        pltpu.VMEM((2, NZ, WIRE, 128), BF16),
        pltpu.VMEM((4, WIRE, 128), BF16),
        pltpu.VMEM((4, N, N), BF16),
        pltpu.VMEM((NZ, SLAB, N), F32),
        pltpu.VMEM((N, N), F32),
        pltpu.VMEM((2, 8, N), F32),
        pltpu.VMEM((2, 8, N), F32),
        pltpu.VMEM((16, 2, HALF, N), BF16),
        pltpu.VMEM((16, 2, HALF, N), BF16),
        pltpu.VMEM((16, 2, HALF, N), BF16),
        pltpu.VMEM((4, N, N), F32),
        pltpu.VMEM((NZ, WIRE, 128), BF16),
        pltpu.VMEM((NZ, WIRE, 128), BF16),
        pltpu.VMEM((2, NZ, WIRE_ONE, 128), BF16),
        pltpu.VMEM((2, NZ, WIRE_ONE, 128), BF16),
        pltpu.VMEM((SLAB, 8, N), F32),
        pltpu.VMEM((4, SLAB, N), F32),
        pltpu.VMEM((2, WIRE, 128), BF16),
        pltpu.VMEM((2 * NZ, 8, BANDS), F32),
        pltpu.VMEM((4, 4, 8, BANDS), F32),
        pltpu.VMEM((BANDS, BANDS), F32),
        pltpu.VMEM((256, BANDS), BF16),
        pltpu.VMEM((8, SLAB, N), F32),
    ]
    counts = [10, 4, 4, 14, 16, 4, 4, 4, 8, 4, 8, 2, 2, 21, 24, 15, 16, 15, 16] + [3, 12, 16, 16, 16] * 3
    scratch += [dma(n) for n in counts]
    return pl.pallas_call(
        kernel,
        out_shape=(
            jax.ShapeDtypeStruct((8, SLAB, N), BF16),
            jax.ShapeDtypeStruct((8, SLAB, N), F32),
        ),
        in_specs=[hbm] * 10,
        out_specs=(vmem, vmem),
        scratch_shapes=scratch,
        compiler_params=pltpu.CompilerParams(
            collective_id=0, has_side_effects=True, vmem_limit_bytes=64 << 20
        ),
        cost_estimate=pl.CostEstimate(
            flops=4 * 64 * 2 * N**3, bytes_accessed=4 << 20, transcendentals=0
        ),
    )(*arguments, jnp.asarray(table), jnp.asarray(np.ascontiguousarray(table.T)))


def solution(mesh):
    return jax.shard_map(
        on_device,
        mesh=mesh,
        in_specs=(
            P(("grp", "band"), "ga", None),
            P("band", "ga", None),
            P("band", "ga", None),
            P("band"),
            P("band"),
            P("ga", None),
            P(None, "ga", None),
            P(None, "ga"),
        ),
        out_specs=(P("band", "ga", None), P("band", "ga", None)),
        check_vma=False,
    )
```

```python
import functools

import jax
import jax.numpy as jnp
import ml_dtypes
import numpy as np
from jax import lax
from jax.experimental import pallas as pl
from jax.experimental.pallas import tpu as pltpu
from jax.sharding import PartitionSpec as P

EXCHANGE_FRACTION = 0.25
F32, BF16 = jnp.float32, jnp.bfloat16
MESH = pl.DeviceIdType.MESH
N = 192
NZ = 8
SLAB = N // NZ
HALF = N // 2
BANDS = 128


def cosine_table(length):
    rows = np.arange(length, dtype=np.float32)[:, None]
    cols = np.arange(length, dtype=np.float32)[None]
    one, two = np.sqrt(np.float32(1.0 / length)), np.sqrt(np.float32(2.0 / length))
    factor = np.where(rows == 0, one, two).astype(np.float32)
    angle = np.float32(np.pi) * (cols + np.float32(0.5)) * rows / np.float32(length)
    return (factor * np.cos(angle)).astype(ml_dtypes.bfloat16)


def split_wires(first, second):
    first, second = first[: 3 * SLAB], second[: 3 * SLAB]
    return jnp.concatenate([first, second[:8]], axis=0), second[8:]


def join_wires(long, short):
    return jnp.concatenate([long[3 * SLAB :], short], axis=0)


def pack_one(slab):
    ends = slab[:, 128:]
    ends = jnp.concatenate(
        [
            jnp.concatenate([ends[:8], ends[8:16]], axis=1),
            jnp.concatenate([ends[16:], jnp.zeros((8, 64), F32)], axis=1),
        ],
        axis=0,
    )
    unused = jnp.zeros((WIRE_ONE - SLAB - 16, 128), F32)
    return jnp.concatenate([slab[:, :128], ends, unused], axis=0).astype(BF16)


def unpack_one(wire):
    value = wire.astype(F32)
    ends = value[SLAB : SLAB + 16]
    ends = jnp.concatenate([ends[:8, :64], ends[:8, 64:], ends[8:, :64]], axis=0)
    return [jnp.concatenate([value[:SLAB], ends], axis=1)]


def pack_half(half):
    ends = jnp.concatenate([half[: HALF // 2, 128:], half[HALF // 2 :, 128:]], axis=1)
    return jnp.concatenate([half[:, :128], ends], axis=0).astype(BF16)


def unpack_half(wire):
    value = wire.astype(F32)
    ends = jnp.concatenate([value[HALF:, :64], value[HALF:, 64:]], axis=0)
    return jnp.concatenate([value[:HALF], ends], axis=1)


def tree_sum(terms):
    while len(terms) > 1:
        terms = [a + b for a, b in zip(terms[::2], terms[1::2])] + terms[len(terms) & ~1 :]
    return terms[0]


def inverse_factor(gram, halfway):
    lane = lax.broadcasted_iota(jnp.int32, (8, BANDS), 1)
    sub = lax.broadcasted_iota(jnp.int32, (8, BANDS), 0)
    count = BANDS // 8
    blocks = [gram[8 * i : 8 * i + 8, :] for i in range(count)]
    done = []
    for b in range(count):
        if b == 9:
            halfway()
        k0 = 8 * b
        inside = (lane >= k0) & (lane < k0 + 8)
        rows = [jnp.broadcast_to(blocks[b][t : t + 1, :], (8, BANDS)) for t in range(8)]
        a = [
            [jnp.broadcast_to(rows[t][:, k0 + s : k0 + s + 1], (8, BANDS)) for s in range(t + 1)]
            for t in range(8)
        ]
        low = [[None] * 8 for _ in range(8)]
        rinv = [None] * 8
        for t in range(8):
            rinv[t] = lax.rsqrt(a[t][t])
            for u in range(t + 1, 8):
                low[u][t] = a[u][t] * rinv[t]
            for u in range(t + 1, 8):
                for s in range(t + 1, u + 1):
                    a[u][s] = a[u][s] - low[u][t] * low[s][t]
        inv = [[None] * 8 for _ in range(8)]
        for s in range(8):
            inv[s][s] = rinv[s]
            for t in range(s + 1, 8):
                acc = tree_sum([low[t][u] * inv[u][s] for u in range(s, t)])
                inv[t][s] = -(acc * rinv[t])
        unit = [
            jnp.where(lane == k0 + t, 1.0, jnp.where(inside, 0.0, rows[t])) for t in range(8)
        ]
        panel = [tree_sum([inv[t][s] * unit[s] for s in range(t + 1)]) for t in range(8)]
        packed = panel[0]
        for t in range(1, 8):
            packed = jnp.where(sub == t, panel[t], packed)
        done.append(jnp.where(lane <= sub + k0, packed, 0.0))
        for i in range(b + 1, count):
            column = [
                jnp.broadcast_to(blocks[i][:, k0 + s : k0 + s + 1], (8, BANDS)) for s in range(8)
            ]
            new = jnp.where(inside, 0.0, blocks[i])
            factor = [tree_sum([inv[t][s] * column[s] for s in range(t + 1)]) for t in range(8)]
            blocks[i] = new - tree_sum([factor[t] * panel[t] for t in range(8)])
    return jnp.concatenate(done, axis=0)


def split_bf16(value):
    first = value.astype(BF16)
    rest = value - first.astype(F32)
    second = rest.astype(BF16)
    third = (rest - second.astype(F32)).astype(BF16)
    return [first.astype(F32), second.astype(F32), third.astype(F32)]


def mod4(i):
    return lax.rem(i, 4)


class PlaneGather:
    def __init__(self, place, ref, first, second, sib, got, got_sib):
        self.place, self.ref = place, ref
        self.s_first, self.s_second, self.s_sib = first, second, sib
        self.r_ici, self.r_sib = got, got_sib

    def slot(self, d, e):
        p = self.place
        f, s = mod4(p.f + d), mod4(p.s + e)
        return (1 - p.c) * (4 * s + f) + p.c * (4 * f + s)

    def peer(self, d, e):
        p = self.place
        f, s = mod4(p.f + d), mod4(p.s + e)
        return p.dev((1 - p.c) * f + p.c * s, (1 - p.c) * s + p.c * f, p.z, p.c)

    def copy(self, sl, half, send, recv, device):
        part = self.ref.at[sl, half]
        return pltpu.make_async_remote_copy(
            src_ref=part,
            dst_ref=part,
            send_sem=send,
            recv_sem=recv,
            device_id=device,
            device_id_type=MESH,
        )

    def first_copy(self, d):
        sl = self.slot(0, 0)
        return self.copy(sl, self.place.c, self.s_first.at[d - 1], self.r_ici.at[sl], self.peer(d, 0))

    def second_copy(self, d, e):
        sl = self.slot(d, 0)
        return self.copy(
            sl, self.place.c, self.s_second.at[3 * d + e - 1], self.r_ici.at[sl], self.peer(0, e)
        )

    def sib_copy(self, d, e):
        p = self.place
        sl = self.slot(d, e)
        return self.copy(sl, p.c, self.s_sib.at[4 * d + e], self.r_sib.at[sl], p.sibling)

    def start(self):
        for d in (1, 3, 2):
            self.first_copy(d).start()
        for e in (1, 3, 2):
            self.second_copy(0, e).start()
        self.sib_copy(0, 0).start()

    def forward(self):
        for d in (1, 3, 2):
            sl = self.slot(d, 0)
            self.copy(
                sl, self.place.c, self.s_first.at[0], self.r_ici.at[sl], self.peer(d, 0)
            ).wait_recv()
            for e in (1, 3, 2):
                self.second_copy(d, e).start()
            self.sib_copy(d, 0).start()

    def hand_on(self, offsets):
        for d, e in offsets:
            sl = self.slot(d, e)
            self.copy(
                sl, self.place.c, self.s_first.at[0], self.r_ici.at[sl], self.peer(0, e)
            ).wait_recv()
            self.sib_copy(d, e).start()

    def wait_sib(self, sl):
        p = self.place
        self.copy(sl, 1 - p.c, self.s_sib.at[0], self.r_sib.at[sl], p.sibling).wait_recv()

    def finish(self):
        for d in (1, 2, 3):
            self.first_copy(d).wait_send()
        for d in range(4):
            for e in (1, 2, 3):
                self.second_copy(d, e).wait_send()
        for d in range(4):
            for e in range(4):
                self.sib_copy(d, e).wait_send()


class Place:
    def __init__(self):
        self.g = lax.axis_index("grp")
        self.b = lax.axis_index("band")
        self.z = lax.axis_index("ga")
        self.x = lax.div(self.b, 4)
        self.y_lo = lax.rem(lax.div(self.b, 2), 2)
        self.c = lax.rem(self.b, 2)
        self.y = 2 * self.g + self.y_lo
        self.f = (1 - self.c) * self.x + self.c * self.y
        self.s = (1 - self.c) * self.y + self.c * self.x
        self.sibling = self.dev(self.x, self.y, self.z, 1 - self.c)

    def dev(self, x, y, z, c):
        return {"grp": lax.div(y, 2), "band": 4 * x + 2 * lax.rem(y, 2) + c, "ga": z}

    def z_peer(self, d, c):
        return self.dev(self.x, self.y, lax.rem(self.z + d, NZ), c)


def remote(src, dst, send, recv, device):
    return pltpu.make_async_remote_copy(
        src_ref=src,
        dst_ref=dst,
        send_sem=send,
        recv_sem=recv,
        device_id=device,
        device_id_type=MESH,
    )


Z_ORDER = (4, 3, 5, 2, 6, 1, 7)
NEAR = ((0, 1), (0, 3), (0, 2))
CROSS = ((0, 0), (1, 0), (0, 1), (3, 0), (0, 3), (2, 0), (0, 2))
LATE = ((1, 1), (1, 3), (3, 1), (3, 3), (1, 2), (2, 1), (3, 2), (2, 3), (2, 2))
WIRE_ONE = 48
WIRE = 80


def pack(pair):
    ends = jnp.concatenate([pair[:SLAB, 128:], pair[SLAB:, 128:]], axis=1)
    unused = jnp.zeros((WIRE - 3 * SLAB, 128), F32)
    return jnp.concatenate([pair[:, :128], ends, unused], axis=0).astype(BF16)


def unpack(wire):
    value = wire.astype(F32)
    ends = value[2 * SLAB : 3 * SLAB]
    return [
        jnp.concatenate([value[:SLAB], ends[:, :64]], axis=1),
        jnp.concatenate([value[SLAB : 2 * SLAB], ends[:, 64:]], axis=1),
    ]


def kernel(
    occ_hbm,
    resp_hbm,
    ground_hbm,
    index_hbm,
    energy_hbm,
    local_hbm,
    field_hbm,
    table_hbm,
    c_hbm,
    ct_hbm,
    proj_ref,
    res_ref,
    occ_ref,
    resp_ref,
    ground_ref,
    index_ref,
    energy_ref,
    local_ref,
    field_ref,
    c_ref,
    ct_ref,
    occ_src,
    occ_got,
    resp_long,
    resp_short,
    sib_long,
    sib_short,
    exch_sib,
    resp_full,
    table_got,
    table,
    halo_src,
    halo_got,
    occ_all,
    occ_full,
    resp_all,
    exch_all,
    total,
    rs_src,
    rs_got,
    rows32,
    exch_own,
    exch_wire,
    gram_z,
    gram_xy,
    gram_full,
    spread,
    proj32,
    *sems,
):
    p = Place()
    z, c, x, y, g = p.z, p.c, p.x, p.y, p.g
    sems = list(sems)
    take = lambda: sems.pop(0)
    in_s = take()
    occ_s, occ_r = take(), take()
    resp_s, resp_r = take(), take()
    sib_s, sib_r = take(), take()
    table_s, table_r = take(), take()
    table_sib_s = take()
    halo_s, halo_r = take(), take()
    rs_s, rs_r = take(), take()
    gz_s, gz_r = take(), take()
    gp_s, gp_r = take(), take()
    occ_gather = PlaneGather(p, occ_all, *[take() for _ in range(5)])
    resp_gather = PlaneGather(p, resp_all, *[take() for _ in range(5)])
    exch_gather = PlaneGather(p, exch_all, *[take() for _ in range(5)])

    loads = [
        pltpu.make_async_copy(src, dst, in_s.at[i])
        for i, (src, dst) in enumerate(
            (
                (occ_hbm, occ_ref),
                (resp_hbm, resp_ref),
                (table_hbm, table_got.at[z]),
                (c_hbm, c_ref),
                (ct_hbm, ct_ref),
                (ground_hbm, ground_ref),
                (field_hbm, field_ref),
                (local_hbm, local_ref),
                (index_hbm, index_ref),
                (energy_hbm, energy_ref),
            )
        )
    ]
    for load in loads:
        load.start()

    barrier = pltpu.get_barrier_semaphore()
    peers = [p.z_peer(d, k) for d in range(1, NZ) for k in (0, 1)]
    peers += [p.sibling, p.dev(x, p.y + 1 - 2 * p.y_lo, z, 1 - c)]
    plane = [(d, e) for d in (2, 1, 3, 0) for e in (2, 1, 3, 0) if (d, e) != (0, 0)]
    peers += [p.dev(mod4(x + d), mod4(y + e), z, c) for d, e in plane]
    for peer in peers:
        pl.semaphore_signal(barrier, inc=1, device_id=peer, device_id_type=MESH)

    for load in loads[:3]:
        load.wait()
    for r in range(4):
        occ_src[r] = pack_one(occ_ref[r].astype(F32))
    wires = []
    for h in range(2):
        pair = [resp_ref[4 * g + 2 * h + r].astype(F32) for r in range(2)]
        wires.append(pack(jnp.concatenate(pair, axis=0)).astype(F32))
    for ref, wire in zip((resp_long, resp_short), split_wires(*wires)):
        ref[z] = wire.astype(BF16)
    edge = [resp_ref[j].astype(F32) for j in range(8)]
    halo_src[0] = jnp.concatenate([e[SLAB - 1 : SLAB] for e in edge], axis=0)
    halo_src[1] = jnp.concatenate([e[0:1] for e in edge], axis=0)
    pl.semaphore_wait(barrier, len(peers))

    half_of_z = lax.div(z, 4)
    quarter = lax.rem(z, 4)

    def occ_out(r):
        return remote(
            occ_src.at[r],
            occ_got.at[quarter],
            occ_s.at[r],
            occ_r.at[quarter],
            p.dev(x, y, 4 * c + r, half_of_z),
        )

    def occ_in(q):
        return remote(
            occ_src.at[q],
            occ_got.at[q],
            occ_s.at[q],
            occ_r.at[q],
            p.dev(x, y, 4 * c + q, half_of_z),
        )

    def mine(r):
        return (half_of_z == c) & (quarter == r)

    for r in range(4):
        @pl.when(jnp.logical_not(mine(r)))
        def _():
            occ_out(r).start()

        @pl.when(mine(r))
        def _():
            occ_got[r] = occ_src[r]

    k_table = 2 * p.y_lo + c
    twin = p.y + 1 - 2 * p.y_lo
    mates = [p.sibling, p.dev(x, twin, z, c), p.dev(x, twin, z, 1 - c)]

    def table_slot(d):
        src = lax.rem(z + NZ - d, NZ)
        return table_got.at[src], table_r.at[src]

    def table_copy(i):
        d = k_table + 4 * i
        slot, recv = table_got.at[z], table_r.at[z]
        return remote(slot, slot, table_s.at[i], recv, p.z_peer(d, c))

    def table_on(i, m):
        slot, recv = table_slot(k_table + 4 * i)
        return remote(slot, slot, table_sib_s.at[3 * i + m], recv, mates[m])

    def table_wait(i):
        slot, recv = table_slot(k_table + 4 * i)
        remote(slot, slot, table_s.at[0], recv, p.sibling).wait_recv()
        for m in range(3):
            table_on(i, m).start()

    def table_wait_mates():
        for m in range(1, 4):
            other = lax.rem(k_table + m, 4)

            @pl.when(other > 0)
            def _():
                slot, recv = table_slot(other)
                remote(slot, slot, table_s.at[0], recv, p.sibling).wait_recv()

            slot, recv = table_slot(other + 4)
            remote(slot, slot, table_s.at[0], recv, p.sibling).wait_recv()

    def for_table(act):
        @pl.when(k_table > 0)
        def _():
            act(0)

        act(1)

    resp_got = (resp_long, resp_short)

    def resp_copy(h, d):
        slot = resp_got[h].at[z]
        return remote(
            slot, slot, resp_s.at[7 * h + d - 1], resp_r.at[8 * h + z], p.z_peer(d, c)
        )

    def resp_wait(h, d):
        src = lax.rem(z + d, NZ)
        slot = resp_got[h].at[src]
        remote(slot, slot, resp_s.at[0], resp_r.at[8 * h + src], p.z_peer(d, c)).wait_recv()

    def sib_resp(h):
        return remote(
            resp_got[h].at[z], (sib_long, sib_short)[h], sib_s.at[h], sib_r.at[h], p.sibling
        )

    def two_pairs(long, short):
        long, short = long.astype(F32), short.astype(F32)
        return unpack(long) + unpack(join_wires(long, short))

    def halo_copy(k):
        return remote(
            halo_src.at[k], halo_got.at[k], halo_s.at[k], halo_r.at[k], p.z_peer((1, 7)[k], c)
        )

    for_table(lambda i: table_copy(i).start())
    for d in Z_ORDER:
        resp_copy(0, d).start()
    for d in Z_ORDER:
        resp_copy(1, d).start()
    for h in range(2):
        sib_resp(h).start()
    for k in range(2):
        halo_copy(k).start()

    for q in range(4):
        @pl.when(jnp.logical_not(mine(q)))
        def _():
            occ_in(q).wait_recv()

    own = 4 * y + x
    occ_all[own, c] = pack_half(
        jnp.concatenate([unpack_one(occ_got[q])[0] for q in range(4)], axis=0)
    )
    occ_gather.start()

    def arrange(parts):
        for k in range(8):
            rows32[:, k, :] = parts[k]

    def by_core(mine_part, other_part):
        first = [jnp.where(c == 0, mine_part(r), other_part(r)) for r in range(4)]
        last = [jnp.where(c == 0, other_part(r), mine_part(r)) for r in range(4)]
        return first + last

    def rows_half():
        return rows32[pl.ds((SLAB // 2) * c, SLAB // 2)].reshape(HALF, N).astype(BF16)

    def slab_of(ref):
        def part(r):
            return unpack(ref(r // 2))[r % 2]

        return part

    for h in range(2):
        sib_resp(h).wait_recv()
    ours = two_pairs(resp_long[z], resp_short[z])
    theirs = two_pairs(sib_long[...], sib_short[...])
    arrange(by_core(lambda r: ours[r], lambda r: theirs[r]))
    resp_all[own, c] = rows_half()

    for load in loads[3:]:
        load.wait()
    for_table(table_wait)
    occ_gather.forward()
    occ_gather.hand_on(NEAR)
    table_wait_mates()
    table[...] = table_got[...].reshape(N, N).T

    def whole_bands(h):
        for d in Z_ORDER:
            resp_wait(h, d)
        if h == 0:
            parts = [unpack(resp_long[s]) for s in range(NZ)]
        else:
            parts = [two_pairs(resp_long[s], resp_short[s])[2:] for s in range(NZ)]
        for r in range(2):
            whole = [parts[s][r] for s in range(NZ)]
            resp_full[2 * h + r] = jnp.concatenate(whole, axis=0).astype(BF16)

    whole_bands(0)

    def slot_at(dx, dy):
        return 4 * mod4(y + dy) + mod4(x + dx)

    def receive(sl):
        occ_gather.wait_sib(sl)
        halves = [unpack_half(occ_all[sl, k]) for k in range(2)]
        occ_full[sl] = jnp.concatenate(halves, axis=0).astype(BF16)

    def late_slots(t):
        out = []
        for q in range(3):
            pick = [LATE[3 * i + q] for i in range(3)]
            dx, dy = [
                jnp.where(t == 0, pick[0][k], jnp.where(t == 1, pick[1][k], pick[2][k]))
                for k in range(2)
            ]
            out.append(slot_at(dx, dy))
        return out

    def pairs(slots, bands):
        orbitals = [occ_full[sl] for sl in slots]
        which = [(r, q) for r in bands for q in range(len(slots))]
        first = [
            jnp.dot(orbitals[q] * resp_full[r], ct_ref[...], preferred_element_type=F32).astype(BF16)
            for r, q in which
        ]
        weighted = [
            (jnp.dot(c_ref[...], f, preferred_element_type=F32) * table[...]).astype(BF16)
            for f in first
        ]
        third = [
            jnp.dot(ct_ref[...], w, preferred_element_type=F32).astype(BF16) for w in weighted
        ]
        for r in bands:
            acc = total[r]
            for i, (band, q) in enumerate(which):
                if band is r:
                    potential = jnp.dot(third[i], c_ref[...], preferred_element_type=F32)
                    acc = acc + orbitals[q].astype(F32) * potential
            total[r] = acc

    def rs_copy(h, d):
        to = lax.rem(z + d, NZ)
        return remote(
            rs_src.at[h, to],
            rs_got.at[h, z],
            rs_s.at[7 * h + d - 1],
            rs_r.at[8 * h + z],
            p.z_peer(d, c),
        )

    def reduce_start(h):
        bands = (2 * h, 2 * h + 1)
        for s in range(NZ):
            out = [total[r, SLAB * s : SLAB * s + SLAB, :] * (1.0 / BANDS) for r in bands]
            rs_src[h, s] = pack(jnp.concatenate(out, axis=0))
        for d in Z_ORDER:
            rs_copy(h, d).start()
        start = pl.multiple_of(SLAB * z, 8)
        for r in bands:
            exch_own[r] = total[r, pl.ds(start, SLAB), :] * (1.0 / BANDS)

    def reduce_finish(h):
        bands = (2 * h, 2 * h + 1)
        acc = [exch_own[r] for r in bands]
        for d in Z_ORDER:
            src = lax.rem(z + d, NZ)
            slot = rs_got.at[h, src]
            remote(slot, slot, rs_s.at[0], rs_r.at[8 * h + src], p.z_peer(d, c)).wait_recv()
            acc = [a + b for a, b in zip(acc, unpack(rs_got[h, src]))]
        for r, a in zip(bands, acc):
            exch_own[r] = a

    total[...] = jnp.zeros_like(total)
    near = [slot_at(dx, dy) for dx, dy in CROSS]
    for sl in near:
        receive(sl)

    def near_step(h, carry):
        @pl.when(h == 1)
        def _():
            occ_gather.hand_on(LATE[:3])

        for some in (near[:4], near[4:]):
            pairs(some, (2 * h, 2 * h + 1))
        return carry

    whole_bands(1)
    lax.fori_loop(0, 2, near_step, 0)
    occ_gather.hand_on(LATE[3:])
    resp_gather.start()

    def late_step(i, carry):
        h, t = lax.div(i, 3), lax.rem(i, 3)

        @pl.when(h == 0)
        def _():
            for sl in late_slots(t):
                receive(sl)

        pairs(late_slots(t), (2 * h, 2 * h + 1))

        @pl.when(t == 2)
        def _():
            reduce_start(h)

        @pl.when(i == 4)
        def _():
            resp_gather.forward()
            resp_gather.hand_on(NEAR)

        return carry

    lax.fori_loop(0, 6, late_step, 0)

    resp_gather.hand_on(LATE)
    for k in range(2):
        remote(
            halo_src.at[k], halo_got.at[k], halo_s.at[k], halo_r.at[k], p.z_peer((7, 1)[k], c)
        ).wait_recv()
    for j in range(8):
        band = resp_ref[j].astype(F32)
        above = jnp.concatenate([halo_got[0, j : j + 1, :], band[: SLAB - 1]], axis=0)
        below = jnp.concatenate([band[1:], halo_got[1, j : j + 1, :]], axis=0)
        left = jnp.concatenate([band[:, N - 1 :], band[:, : N - 1]], axis=1)
        right = jnp.concatenate([band[:, 1:], band[:, :1]], axis=1)
        value = 0.5 * (4.0 * band - ((above + below) + left + right))
        value = value + (local_ref[...] - energy_ref[j]) * band
        weights = [jnp.where(index_ref[j] == k, 1.0, 0.0) for k in range(3)]
        perturb = weights[0] * field_ref[0] + weights[1] * field_ref[1] + weights[2] * field_ref[2]
        res_ref[j] = value + perturb * ground_ref[j].astype(F32)

    row = lax.broadcasted_iota(jnp.int32, (256, BANDS), 0)
    col = lax.broadcasted_iota(jnp.int32, (256, BANDS), 1)
    chip, member = row // 16, row % 8
    chip_x, chip_y = chip % 4, chip // 4
    natural = 32 * chip_x + 16 * (chip_y % 2) + 8 * (member // 4) + 4 * (chip_y // 2) + member % 4
    spread[...] = jnp.where(natural == col, 1.0, 0.0).astype(BF16)
    parity = (lax.broadcasted_iota(jnp.int32, (8, 256), 1) // 8) % 2

    for r in range(4):
        @pl.when(jnp.logical_not(mine(r)))
        def _():
            occ_out(r).wait_send()

    for_table(lambda i: table_copy(i).wait_send())
    for m in range(3):
        for_table(lambda i: table_on(i, m).wait_send())
    for h in range(2):
        for d in range(1, NZ):
            resp_copy(h, d).wait_send()
        sib_resp(h).wait_send()
        halo_copy(h).wait_send()
    occ_gather.finish()

    for s in range(16):
        resp_gather.wait_sib(s)

    def sib_exch(h):
        return remote(exch_wire.at[h], exch_sib.at[h], sib_s.at[2 + h], sib_r.at[2 + h], p.sibling)

    def sib_exch_start(h):
        exch_wire[h] = pack(jnp.concatenate([exch_own[2 * h], exch_own[2 * h + 1]], axis=0))
        sib_exch(h).start()

    reduce_finish(0)
    sib_exch_start(0)
    reduce_finish(1)
    sib_exch_start(1)

    zero = jnp.zeros((SLAB, N), F32)
    own_part = slab_of(lambda h: exch_wire[h])
    arrange(by_core(own_part, lambda r: zero))
    left_rows = rows32[...].reshape(N, N).astype(BF16)
    part = jnp.zeros((16, 256), F32)
    for a in range(SLAB // 2):
        bands = resp_all[:, a // 6, 16 * (a % 6) : 16 * (a % 6) + 16, :].reshape(256, N)
        part = part + lax.dot_general(
            left_rows[16 * a : 16 * a + 16],
            bands,
            (((1,), (1,)), ((), ())),
            preferred_element_type=F32,
        )
    folded = jnp.where(parity == 0, part[:8], part[8:])
    pieces = jnp.concatenate(split_bf16(folded), axis=0).astype(BF16)
    pieces = jnp.dot(pieces, spread[...], preferred_element_type=F32)
    gram_z[2 * z + c] = (pieces[:8] + pieces[8:16] + pieces[16:24]) * (1.0 / (N * N))

    z_line = [(d, k) for d in Z_ORDER for k in (0, 1)] + [(0, 1)]

    def line_core(k):
        return (1 - k) * c + k * (1 - c)

    def gram_copy(i):
        d, k = z_line[i]
        mine_slot = gram_z.at[2 * z + c]
        return remote(
            mine_slot, mine_slot, gz_s.at[i], gz_r.at[2 * z + c], p.z_peer(d, line_core(k))
        )

    for i in range(len(z_line)):
        gram_copy(i).start()

    for h in range(2):
        sib_exch(h).wait_recv()
    arrange(by_core(own_part, slab_of(lambda h: exch_sib[h])))
    exch_all[own, c] = rows_half()
    exch_gather.start()

    resp_gather.finish()
    for h in range(2):
        sib_exch(h).wait_send()
        for d in range(1, NZ):
            rs_copy(h, d).wait_send()

    for d, k in z_line:
        src = 2 * lax.rem(z + d, NZ) + line_core(k)
        slot = gram_z.at[src]
        remote(slot, slot, gz_s.at[0], gz_r.at[src], p.z_peer(d, line_core(k))).wait_recv()
    summed = gram_z[0]
    for i in range(1, 2 * NZ):
        summed = summed + gram_z[i]
    gram_xy[y, x] = summed

    def gram_plane(i):
        d, e = plane[i]
        slot = gram_xy.at[y, x]
        device = p.dev(mod4(x + d), mod4(y + e), z, c)
        return remote(slot, slot, gp_s.at[i], gp_r.at[own], device)

    for i in range(len(plane)):
        gram_plane(i).start()
    exch_gather.forward()
    exch_gather.hand_on(NEAR)
    for i in range(len(z_line)):
        gram_copy(i).wait_send()
    for d, e in plane:
        src_x, src_y = mod4(x + d), mod4(y + e)
        slot = gram_xy.at[src_y, src_x]
        remote(
            slot, slot, gp_s.at[0], gp_r.at[4 * src_y + src_x], p.dev(src_x, src_y, z, c)
        ).wait_recv()

    for i in range(32):
        n_x, n_lo, n_c, n_g = i // 8, (i // 4) % 2, (i // 2) % 2, i % 2
        gram_full[4 * i : 4 * i + 4, :] = gram_xy[2 * n_g + n_lo, n_x, 4 * n_c : 4 * n_c + 4, :]
    gram = gram_full[...]
    gram_full[...] = inverse_factor(
        0.5 * (gram + gram.T), lambda: exch_gather.hand_on(LATE)
    )
    inverse = gram_full[pl.ds(pl.multiple_of(8 * p.b, 8), 8), :]

    for s in range(16):
        exch_gather.wait_sib(s)

    for half in range(2):
        slot = 4 * (2 * half + p.y_lo) + x
        rows32[...] = exch_all[slot].reshape(SLAB, 8, N).astype(F32)
        for r in range(4):
            value = jnp.where(c == 0, rows32[:, r, :], rows32[:, 4 + r, :])
            res_ref[4 * half + r] = res_ref[4 * half + r] - EXCHANGE_FRACTION * value

    pieces = jnp.concatenate(split_bf16(inverse), axis=0).astype(BF16)
    wide = lax.dot_general(
        pieces, spread[...], (((1,), (1,)), ((), ())), preferred_element_type=F32
    )
    parity = jnp.concatenate([parity] * 3, axis=0)
    left = jnp.concatenate(
        [jnp.where(parity == 0, wide, 0.0), jnp.where(parity == 1, wide, 0.0)], axis=0
    ).astype(BF16)
    for a in range(SLAB // 2):
        vectors = exch_all[:, a // 6, 16 * (a % 6) : 16 * (a % 6) + 16, :].reshape(256, N)
        out = jnp.dot(left, vectors, preferred_element_type=F32)
        for k in range(2):
            o = out[24 * k : 24 * k + 24]
            proj32[:, 2 * a + k, :] = (o[16:24] + o[8:16]) + o[:8]
    for j in range(8):
        proj_ref[j] = proj32[j].astype(BF16)

    for i in range(len(plane)):
        gram_plane(i).wait_send()
    exch_gather.finish()


def on_device(*arguments):
    arguments = arguments[:7] + (arguments[7].T,)
    table = cosine_table(N)
    vmem = pl.BlockSpec(memory_space=pltpu.VMEM)
    hbm = pl.BlockSpec(memory_space=pltpu.HBM)
    dma = lambda n: pltpu.SemaphoreType.DMA((n,))
    scratch = [
        pltpu.VMEM((4, SLAB, N), BF16),
        pltpu.VMEM((8, SLAB, N), BF16),
        pltpu.VMEM((8, SLAB, N), BF16),
        pltpu.SMEM((8,), jnp.int32),
        pltpu.SMEM((8,), F32),
        pltpu.VMEM((SLAB, N), F32),
        pltpu.VMEM((3, SLAB, N), F32),
        pltpu.VMEM((N, N), BF16),
        pltpu.VMEM((N, N), BF16),
        pltpu.VMEM((4, WIRE_ONE, 128), BF16),
        pltpu.VMEM((4, WIRE_ONE, 128), BF16),
        pltpu.VMEM((NZ, WIRE, 128), BF16),
        pltpu.VMEM((NZ, WIRE - 16, 128), BF16),
        pltpu.VMEM((WIRE, 128), BF16),
        pltpu.VMEM((WIRE - 16, 128), BF16),
        pltpu.VMEM((2, WIRE, 128), BF16),
        pltpu.VMEM((4, N, N), BF16),
        pltpu.VMEM((NZ, SLAB, N), F32),
        pltpu.VMEM((N, N), F32),
        pltpu.VMEM((2, 8, N), F32),
        pltpu.VMEM((2, 8, N), F32),
        pltpu.VMEM((16, 2, 3 * HALF // 2, 128), BF16),
        pltpu.VMEM((16, N, N), BF16),
        pltpu.VMEM((16, 2, HALF, N), BF16),
        pltpu.VMEM((16, 2, HALF, N), BF16),
        pltpu.VMEM((4, N, N), F32),
        pltpu.VMEM((2, NZ, WIRE, 128), BF16),
        pltpu.VMEM((2, NZ, WIRE, 128), BF16),
        pltpu.VMEM((SLAB, 8, N), F32),
        pltpu.VMEM((4, SLAB, N), F32),
        pltpu.VMEM((2, WIRE, 128), BF16),
        pltpu.VMEM((2 * NZ, 8, BANDS), F32),
        pltpu.VMEM((4, 4, 8, BANDS), F32),
        pltpu.VMEM((BANDS, BANDS), F32),
        pltpu.VMEM((256, BANDS), BF16),
        pltpu.VMEM((8, SLAB, N), F32),
    ]
    counts = [10, 4, 4, 14, 16, 4, 4, 2, 8, 6, 2, 2, 14, 16, 15, 16, 15, 16] + [3, 12, 16, 16, 16] * 3
    scratch += [dma(n) for n in counts]
    return pl.pallas_call(
        kernel,
        out_shape=(pltpu.VMEM((8, SLAB, N), BF16), pltpu.VMEM((8, SLAB, N), F32)),
        in_specs=[hbm] * 10,
        out_specs=(vmem, vmem),
        scratch_shapes=scratch,
        compiler_params=pltpu.CompilerParams(
            collective_id=0, has_side_effects=True, vmem_limit_bytes=(64 << 20) - (10500 << 10)
        ),
        cost_estimate=pl.CostEstimate(
            flops=4 * 64 * 2 * N**3, bytes_accessed=4 << 20, transcendentals=0
        ),
    )(*arguments, jnp.asarray(table), jnp.asarray(np.ascontiguousarray(table.T)))


def solution(mesh):
    return jax.shard_map(
        on_device,
        mesh=mesh,
        in_specs=(
            P(("grp", "band"), "ga", None),
            P("band", "ga", None),
            P("band", "ga", None),
            P("band"),
            P("band"),
            P("ga", None),
            P(None, "ga", None),
            P(None, "ga"),
        ),
        out_specs=(P("band", "ga", None), P("band", "ga", None)),
        check_vma=False,
    )
```

```python
import functools

import jax
import jax.numpy as jnp
import ml_dtypes
import numpy as np
from jax import lax
from jax.experimental import pallas as pl
from jax.experimental.pallas import tpu as pltpu
from jax.sharding import PartitionSpec as P

EXCHANGE_FRACTION = 0.25
F32, BF16 = jnp.float32, jnp.bfloat16
MESH = pl.DeviceIdType.MESH
N = 192
NZ = 8
SLAB = N // NZ
HALF = N // 2
BANDS = 128


def cosine_table(length):
    rows = np.arange(length, dtype=np.float32)[:, None]
    cols = np.arange(length, dtype=np.float32)[None]
    one, two = np.sqrt(np.float32(1.0 / length)), np.sqrt(np.float32(2.0 / length))
    factor = np.where(rows == 0, one, two).astype(np.float32)
    angle = np.float32(np.pi) * (cols + np.float32(0.5)) * rows / np.float32(length)
    return (factor * np.cos(angle)).astype(ml_dtypes.bfloat16)


def split_wires(first, second):
    first, second = first[: 3 * SLAB], second[: 3 * SLAB]
    return jnp.concatenate([first, second[:8]], axis=0), second[8:]


def join_wires(long, short):
    return jnp.concatenate([long[3 * SLAB :], short], axis=0)


def pack_one(slab):
    ends = slab[:, 128:]
    ends = jnp.concatenate(
        [
            jnp.concatenate([ends[:8], ends[8:16]], axis=1),
            jnp.concatenate([ends[16:], jnp.zeros((8, 64), F32)], axis=1),
        ],
        axis=0,
    )
    unused = jnp.zeros((WIRE_ONE - SLAB - 16, 128), F32)
    return jnp.concatenate([slab[:, :128], ends, unused], axis=0).astype(BF16)


def unpack_one(wire):
    value = wire.astype(F32)
    ends = value[SLAB : SLAB + 16]
    ends = jnp.concatenate([ends[:8, :64], ends[:8, 64:], ends[8:, :64]], axis=0)
    return [jnp.concatenate([value[:SLAB], ends], axis=1)]


def pack_half(half):
    ends = jnp.concatenate([half[: HALF // 2, 128:], half[HALF // 2 :, 128:]], axis=1)
    return jnp.concatenate([half[:, :128], ends], axis=0).astype(BF16)


def unpack_half(wire):
    value = wire.astype(F32)
    ends = jnp.concatenate([value[HALF:, :64], value[HALF:, 64:]], axis=0)
    return jnp.concatenate([value[:HALF], ends], axis=1)


def tree_sum(terms):
    while len(terms) > 1:
        terms = [a + b for a, b in zip(terms[::2], terms[1::2])] + terms[len(terms) & ~1 :]
    return terms[0]


def inverse_factor(gram, halfway):
    lane = lax.broadcasted_iota(jnp.int32, (8, BANDS), 1)
    sub = lax.broadcasted_iota(jnp.int32, (8, BANDS), 0)
    count = BANDS // 8
    blocks = [gram[8 * i : 8 * i + 8, :] for i in range(count)]
    done = []
    for b in range(count):
        if b == 9:
            halfway()
        k0 = 8 * b
        inside = (lane >= k0) & (lane < k0 + 8)
        rows = [jnp.broadcast_to(blocks[b][t : t + 1, :], (8, BANDS)) for t in range(8)]
        a = [
            [jnp.broadcast_to(rows[t][:, k0 + s : k0 + s + 1], (8, BANDS)) for s in range(t + 1)]
            for t in range(8)
        ]
        low = [[None] * 8 for _ in range(8)]
        rinv = [None] * 8
        for t in range(8):
            rinv[t] = lax.rsqrt(a[t][t])
            for u in range(t + 1, 8):
                low[u][t] = a[u][t] * rinv[t]
            for u in range(t + 1, 8):
                for s in range(t + 1, u + 1):
                    a[u][s] = a[u][s] - low[u][t] * low[s][t]
        inv = [[None] * 8 for _ in range(8)]
        for s in range(8):
            inv[s][s] = rinv[s]
            for t in range(s + 1, 8):
                acc = tree_sum([low[t][u] * inv[u][s] for u in range(s, t)])
                inv[t][s] = -(acc * rinv[t])
        unit = [
            jnp.where(lane == k0 + t, 1.0, jnp.where(inside, 0.0, rows[t])) for t in range(8)
        ]
        panel = [tree_sum([inv[t][s] * unit[s] for s in range(t + 1)]) for t in range(8)]
        packed = panel[0]
        for t in range(1, 8):
            packed = jnp.where(sub == t, panel[t], packed)
        done.append(jnp.where(lane <= sub + k0, packed, 0.0))
        for i in range(b + 1, count):
            column = [
                jnp.broadcast_to(blocks[i][:, k0 + s : k0 + s + 1], (8, BANDS)) for s in range(8)
            ]
            new = jnp.where(inside, 0.0, blocks[i])
            factor = [tree_sum([inv[t][s] * column[s] for s in range(t + 1)]) for t in range(8)]
            blocks[i] = new - tree_sum([factor[t] * panel[t] for t in range(8)])
    return jnp.concatenate(done, axis=0)


def split_bf16(value):
    first = value.astype(BF16)
    rest = value - first.astype(F32)
    second = rest.astype(BF16)
    third = (rest - second.astype(F32)).astype(BF16)
    return [first.astype(F32), second.astype(F32), third.astype(F32)]


def mod4(i):
    return lax.rem(i, 4)


class PlaneGather:
    def __init__(self, place, ref, first, second, sib, got, got_sib):
        self.place, self.ref = place, ref
        self.s_first, self.s_second, self.s_sib = first, second, sib
        self.r_ici, self.r_sib = got, got_sib

    def slot(self, d, e):
        p = self.place
        f, s = mod4(p.f + d), mod4(p.s + e)
        return (1 - p.c) * (4 * s + f) + p.c * (4 * f + s)

    def peer(self, d, e):
        p = self.place
        f, s = mod4(p.f + d), mod4(p.s + e)
        return p.dev((1 - p.c) * f + p.c * s, (1 - p.c) * s + p.c * f, p.z, p.c)

    def copy(self, sl, half, send, recv, device):
        part = self.ref.at[sl, half]
        return pltpu.make_async_remote_copy(
            src_ref=part,
            dst_ref=part,
            send_sem=send,
            recv_sem=recv,
            device_id=device,
            device_id_type=MESH,
        )

    def first_copy(self, d):
        sl = self.slot(0, 0)
        return self.copy(sl, self.place.c, self.s_first.at[d - 1], self.r_ici.at[sl], self.peer(d, 0))

    def second_copy(self, d, e):
        sl = self.slot(d, 0)
        return self.copy(
            sl, self.place.c, self.s_second.at[3 * d + e - 1], self.r_ici.at[sl], self.peer(0, e)
        )

    def sib_copy(self, d, e):
        p = self.place
        sl = self.slot(d, e)
        return self.copy(sl, p.c, self.s_sib.at[4 * d + e], self.r_sib.at[sl], p.sibling)

    def start(self):
        for d in (1, 3, 2):
            self.first_copy(d).start()
        for e in (1, 3, 2):
            self.second_copy(0, e).start()
        self.sib_copy(0, 0).start()

    def forward(self):
        for d in (1, 3, 2):
            sl = self.slot(d, 0)
            self.copy(
                sl, self.place.c, self.s_first.at[0], self.r_ici.at[sl], self.peer(d, 0)
            ).wait_recv()
            for e in (1, 3, 2):
                self.second_copy(d, e).start()
            self.sib_copy(d, 0).start()

    def hand_on(self, offsets):
        for d, e in offsets:
            sl = self.slot(d, e)
            self.copy(
                sl, self.place.c, self.s_first.at[0], self.r_ici.at[sl], self.peer(0, e)
            ).wait_recv()
            self.sib_copy(d, e).start()

    def wait_sib(self, sl):
        p = self.place
        self.copy(sl, 1 - p.c, self.s_sib.at[0], self.r_sib.at[sl], p.sibling).wait_recv()

    def finish(self):
        for d in (1, 2, 3):
            self.first_copy(d).wait_send()
        for d in range(4):
            for e in (1, 2, 3):
                self.second_copy(d, e).wait_send()
        for d in range(4):
            for e in range(4):
                self.sib_copy(d, e).wait_send()


class Place:
    def __init__(self):
        self.g = lax.axis_index("grp")
        self.b = lax.axis_index("band")
        self.z = lax.axis_index("ga")
        self.x = lax.div(self.b, 4)
        self.y_lo = lax.rem(lax.div(self.b, 2), 2)
        self.c = lax.rem(self.b, 2)
        self.y = 2 * self.g + self.y_lo
        self.f = (1 - self.c) * self.x + self.c * self.y
        self.s = (1 - self.c) * self.y + self.c * self.x
        self.sibling = self.dev(self.x, self.y, self.z, 1 - self.c)

    def dev(self, x, y, z, c):
        return {"grp": lax.div(y, 2), "band": 4 * x + 2 * lax.rem(y, 2) + c, "ga": z}

    def z_peer(self, d, c):
        return self.dev(self.x, self.y, lax.rem(self.z + d, NZ), c)


def remote(src, dst, send, recv, device):
    return pltpu.make_async_remote_copy(
        src_ref=src,
        dst_ref=dst,
        send_sem=send,
        recv_sem=recv,
        device_id=device,
        device_id_type=MESH,
    )


Z_ORDER = (4, 3, 5, 2, 6, 1, 7)
NEAR = ((0, 1), (0, 3), (0, 2))
CROSS = ((0, 0), (1, 0), (0, 1), (3, 0), (0, 3), (2, 0), (0, 2))
LATE = ((1, 1), (1, 3), (3, 1), (3, 3), (1, 2), (2, 1), (3, 2), (2, 3), (2, 2))
WIRE_ONE = 48
WIRE = 80


def pack(pair):
    ends = jnp.concatenate([pair[:SLAB, 128:], pair[SLAB:, 128:]], axis=1)
    unused = jnp.zeros((WIRE - 3 * SLAB, 128), F32)
    return jnp.concatenate([pair[:, :128], ends, unused], axis=0).astype(BF16)


def unpack(wire):
    value = wire.astype(F32)
    ends = value[2 * SLAB : 3 * SLAB]
    return [
        jnp.concatenate([value[:SLAB], ends[:, :64]], axis=1),
        jnp.concatenate([value[SLAB : 2 * SLAB], ends[:, 64:]], axis=1),
    ]


def kernel(
    occ_hbm,
    resp_hbm,
    ground_hbm,
    index_hbm,
    energy_hbm,
    local_hbm,
    field_hbm,
    table_hbm,
    c_hbm,
    ct_hbm,
    proj_ref,
    res_ref,
    occ_ref,
    resp_ref,
    ground_ref,
    index_ref,
    energy_ref,
    local_ref,
    field_ref,
    c_ref,
    ct_ref,
    occ_src,
    occ_got,
    resp_long,
    resp_short,
    sib_long,
    sib_short,
    exch_sib,
    resp_full,
    table_got,
    table,
    halo_src,
    halo_got,
    occ_all,
    occ_full,
    resp_all,
    exch_all,
    total,
    rs_src,
    rs_got,
    rows32,
    exch_own,
    exch_wire,
    gram_z,
    gram_xy,
    gram_full,
    spread,
    proj32,
    *sems,
):
    p = Place()
    z, c, x, y, g = p.z, p.c, p.x, p.y, p.g
    sems = list(sems)
    take = lambda: sems.pop(0)
    in_s = take()
    occ_s, occ_r = take(), take()
    resp_s, resp_r = take(), take()
    sib_s, sib_r = take(), take()
    table_s, table_r = take(), take()
    table_sib_s = take()
    halo_s, halo_r = take(), take()
    rs_s, rs_r = take(), take()
    gz_s, gz_r = take(), take()
    gp_s, gp_r = take(), take()
    occ_gather = PlaneGather(p, occ_all, *[take() for _ in range(5)])
    resp_gather = PlaneGather(p, resp_all, *[take() for _ in range(5)])
    exch_gather = PlaneGather(p, exch_all, *[take() for _ in range(5)])

    loads = [
        pltpu.make_async_copy(src, dst, in_s.at[i])
        for i, (src, dst) in enumerate(
            (
                (occ_hbm, occ_ref),
                (resp_hbm, resp_ref),
                (table_hbm, table_got.at[z]),
                (c_hbm, c_ref),
                (ct_hbm, ct_ref),
                (ground_hbm, ground_ref),
                (field_hbm, field_ref),
                (local_hbm, local_ref),
                (index_hbm, index_ref),
                (energy_hbm, energy_ref),
            )
        )
    ]
    for load in loads:
        load.start()

    barrier = pltpu.get_barrier_semaphore()
    peers = [p.z_peer(d, k) for d in range(1, NZ) for k in (0, 1)]
    peers += [p.sibling, p.dev(x, p.y + 1 - 2 * p.y_lo, z, 1 - c)]
    plane = [(d, e) for d in (2, 1, 3, 0) for e in (2, 1, 3, 0) if (d, e) != (0, 0)]
    peers += [p.dev(mod4(x + d), mod4(y + e), z, c) for d, e in plane]
    for peer in peers:
        pl.semaphore_signal(barrier, inc=1, device_id=peer, device_id_type=MESH)

    for load in loads[:3]:
        load.wait()
    for r in range(4):
        occ_src[r] = pack_one(occ_ref[r].astype(F32))
    wires = []
    for h in range(2):
        pair = [resp_ref[4 * g + 2 * h + r].astype(F32) for r in range(2)]
        wires.append(pack(jnp.concatenate(pair, axis=0)).astype(F32))
    for ref, wire in zip((resp_long, resp_short), split_wires(*wires)):
        ref[z] = wire.astype(BF16)
    edge = [resp_ref[j].astype(F32) for j in range(8)]
    halo_src[0] = jnp.concatenate([e[SLAB - 1 : SLAB] for e in edge], axis=0)
    halo_src[1] = jnp.concatenate([e[0:1] for e in edge], axis=0)
    pl.semaphore_wait(barrier, len(peers))

    half_of_z = lax.div(z, 4)
    quarter = lax.rem(z, 4)

    def occ_out(r):
        return remote(
            occ_src.at[r],
            occ_got.at[quarter],
            occ_s.at[r],
            occ_r.at[quarter],
            p.dev(x, y, 4 * c + r, half_of_z),
        )

    def occ_in(q):
        return remote(
            occ_src.at[q],
            occ_got.at[q],
            occ_s.at[q],
            occ_r.at[q],
            p.dev(x, y, 4 * c + q, half_of_z),
        )

    def mine(r):
        return (half_of_z == c) & (quarter == r)

    for r in range(4):
        @pl.when(jnp.logical_not(mine(r)))
        def _():
            occ_out(r).start()

        @pl.when(mine(r))
        def _():
            occ_got[r] = occ_src[r]

    k_table = 2 * p.y_lo + c
    twin = p.y + 1 - 2 * p.y_lo
    mates = [p.sibling, p.dev(x, twin, z, c), p.dev(x, twin, z, 1 - c)]

    def table_slot(d):
        src = lax.rem(z + NZ - d, NZ)
        return table_got.at[src], table_r.at[src]

    def table_copy(i):
        d = k_table + 4 * i
        slot, recv = table_got.at[z], table_r.at[z]
        return remote(slot, slot, table_s.at[i], recv, p.z_peer(d, c))

    def table_on(i, m):
        slot, recv = table_slot(k_table + 4 * i)
        return remote(slot, slot, table_sib_s.at[3 * i + m], recv, mates[m])

    def table_wait(i):
        slot, recv = table_slot(k_table + 4 * i)
        remote(slot, slot, table_s.at[0], recv, p.sibling).wait_recv()
        for m in range(3):
            table_on(i, m).start()

    def table_wait_mates():
        for m in range(1, 4):
            other = lax.rem(k_table + m, 4)

            @pl.when(other > 0)
            def _():
                slot, recv = table_slot(other)
                remote(slot, slot, table_s.at[0], recv, p.sibling).wait_recv()

            slot, recv = table_slot(other + 4)
            remote(slot, slot, table_s.at[0], recv, p.sibling).wait_recv()

    def for_table(act):
        @pl.when(k_table > 0)
        def _():
            act(0)

        act(1)

    resp_got = (resp_long, resp_short)

    def resp_copy(h, d):
        slot = resp_got[h].at[z]
        return remote(
            slot, slot, resp_s.at[7 * h + d - 1], resp_r.at[8 * h + z], p.z_peer(d, c)
        )

    def resp_wait(h, d):
        src = lax.rem(z + d, NZ)
        slot = resp_got[h].at[src]
        remote(slot, slot, resp_s.at[0], resp_r.at[8 * h + src], p.z_peer(d, c)).wait_recv()

    def sib_resp(h):
        return remote(
            resp_got[h].at[z], (sib_long, sib_short)[h], sib_s.at[h], sib_r.at[h], p.sibling
        )

    def two_pairs(long, short):
        long, short = long.astype(F32), short.astype(F32)
        return unpack(long) + unpack(join_wires(long, short))

    def halo_copy(k):
        return remote(
            halo_src.at[k], halo_got.at[k], halo_s.at[k], halo_r.at[k], p.z_peer((1, 7)[k], c)
        )

    for_table(lambda i: table_copy(i).start())
    for d in Z_ORDER:
        resp_copy(0, d).start()
    for d in Z_ORDER:
        resp_copy(1, d).start()
    for h in range(2):
        sib_resp(h).start()
    for k in range(2):
        halo_copy(k).start()

    for q in range(4):
        @pl.when(jnp.logical_not(mine(q)))
        def _():
            occ_in(q).wait_recv()

    own = 4 * y + x
    occ_all[own, c] = pack_half(
        jnp.concatenate([unpack_one(occ_got[q])[0] for q in range(4)], axis=0)
    )
    occ_gather.start()

    def arrange(parts):
        for k in range(8):
            rows32[:, k, :] = parts[k]

    def by_core(mine_part, other_part):
        first = [jnp.where(c == 0, mine_part(r), other_part(r)) for r in range(4)]
        last = [jnp.where(c == 0, other_part(r), mine_part(r)) for r in range(4)]
        return first + last

    def rows_half():
        return rows32[pl.ds((SLAB // 2) * c, SLAB // 2)].reshape(HALF, N).astype(BF16)

    def slab_of(ref):
        def part(r):
            return unpack(ref(r // 2))[r % 2]

        return part

    for h in range(2):
        sib_resp(h).wait_recv()
    ours = two_pairs(resp_long[z], resp_short[z])
    theirs = two_pairs(sib_long[...], sib_short[...])
    arrange(by_core(lambda r: ours[r], lambda r: theirs[r]))
    resp_all[own, c] = rows_half()

    for load in loads[3:]:
        load.wait()
    for_table(table_wait)
    occ_gather.forward()
    occ_gather.hand_on(NEAR)
    resp_gather.start()
    table_wait_mates()
    table[...] = table_got[...].reshape(N, N).T

    def whole_bands(h):
        for d in Z_ORDER:
            resp_wait(h, d)
        if h == 0:
            parts = [unpack(resp_long[s]) for s in range(NZ)]
        else:
            parts = [two_pairs(resp_long[s], resp_short[s])[2:] for s in range(NZ)]
        for r in range(2):
            whole = [parts[s][r] for s in range(NZ)]
            resp_full[2 * h + r] = jnp.concatenate(whole, axis=0).astype(BF16)

    whole_bands(0)

    def slot_at(dx, dy):
        return 4 * mod4(y + dy) + mod4(x + dx)

    def receive(sl):
        occ_gather.wait_sib(sl)
        halves = [unpack_half(occ_all[sl, k]) for k in range(2)]
        occ_full[sl] = jnp.concatenate(halves, axis=0).astype(BF16)

    def late_slots(t):
        out = []
        for q in range(3):
            pick = [LATE[3 * i + q] for i in range(3)]
            dx, dy = [
                jnp.where(t == 0, pick[0][k], jnp.where(t == 1, pick[1][k], pick[2][k]))
                for k in range(2)
            ]
            out.append(slot_at(dx, dy))
        return out

    def pairs(slots, bands):
        orbitals = [occ_full[sl] for sl in slots]
        which = [(r, q) for r in bands for q in range(len(slots))]
        first = [
            jnp.dot(orbitals[q] * resp_full[r], ct_ref[...], preferred_element_type=F32).astype(BF16)
            for r, q in which
        ]
        weighted = [
            (jnp.dot(c_ref[...], f, preferred_element_type=F32) * table[...]).astype(BF16)
            for f in first
        ]
        third = [
            jnp.dot(ct_ref[...], w, preferred_element_type=F32).astype(BF16) for w in weighted
        ]
        for r in bands:
            acc = total[r]
            for i, (band, q) in enumerate(which):
                if band is r:
                    potential = jnp.dot(third[i], c_ref[...], preferred_element_type=F32)
                    acc = acc + orbitals[q].astype(F32) * potential
            total[r] = acc

    def rs_copy(h, d):
        to = lax.rem(z + d, NZ)
        return remote(
            rs_src.at[h, to],
            rs_got.at[h, z],
            rs_s.at[7 * h + d - 1],
            rs_r.at[8 * h + z],
            p.z_peer(d, c),
        )

    def reduce_start(h):
        bands = (2 * h, 2 * h + 1)
        for s in range(NZ):
            out = [total[r, SLAB * s : SLAB * s + SLAB, :] * (1.0 / BANDS) for r in bands]
            rs_src[h, s] = pack(jnp.concatenate(out, axis=0))
        for d in Z_ORDER:
            rs_copy(h, d).start()
        start = pl.multiple_of(SLAB * z, 8)
        for r in bands:
            exch_own[r] = total[r, pl.ds(start, SLAB), :] * (1.0 / BANDS)

    def reduce_finish(h):
        bands = (2 * h, 2 * h + 1)
        acc = [exch_own[r] for r in bands]
        for d in Z_ORDER:
            src = lax.rem(z + d, NZ)
            slot = rs_got.at[h, src]
            remote(slot, slot, rs_s.at[0], rs_r.at[8 * h + src], p.z_peer(d, c)).wait_recv()
            acc = [a + b for a, b in zip(acc, unpack(rs_got[h, src]))]
        for r, a in zip(bands, acc):
            exch_own[r] = a

    total[...] = jnp.zeros_like(total)
    near = [slot_at(dx, dy) for dx, dy in CROSS]
    for sl in near:
        receive(sl)

    def near_step(h, carry):
        @pl.when(h == 1)
        def _():
            occ_gather.hand_on(LATE[:3])

        for some in (near[:4], near[4:]):
            pairs(some, (2 * h, 2 * h + 1))
        return carry

    whole_bands(1)
    lax.fori_loop(0, 2, near_step, 0)
    occ_gather.hand_on(LATE[3:])

    def late_step(i, carry):
        h, t = lax.div(i, 3), lax.rem(i, 3)

        @pl.when(h == 0)
        def _():
            for sl in late_slots(t):
                receive(sl)

        pairs(late_slots(t), (2 * h, 2 * h + 1))

        @pl.when(t == 2)
        def _():
            reduce_start(h)

        @pl.when(i == 2)
        def _():
            resp_gather.forward()
            resp_gather.hand_on(NEAR)

        return carry

    lax.fori_loop(0, 6, late_step, 0)

    resp_gather.hand_on(LATE)
    for k in range(2):
        remote(
            halo_src.at[k], halo_got.at[k], halo_s.at[k], halo_r.at[k], p.z_peer((7, 1)[k], c)
        ).wait_recv()
    for j in range(8):
        band = resp_ref[j].astype(F32)
        above = jnp.concatenate([halo_got[0, j : j + 1, :], band[: SLAB - 1]], axis=0)
        below = jnp.concatenate([band[1:], halo_got[1, j : j + 1, :]], axis=0)
        left = jnp.concatenate([band[:, N - 1 :], band[:, : N - 1]], axis=1)
        right = jnp.concatenate([band[:, 1:], band[:, :1]], axis=1)
        value = 0.5 * (4.0 * band - ((above + below) + left + right))
        value = value + (local_ref[...] - energy_ref[j]) * band
        weights = [jnp.where(index_ref[j] == k, 1.0, 0.0) for k in range(3)]
        perturb = weights[0] * field_ref[0] + weights[1] * field_ref[1] + weights[2] * field_ref[2]
        res_ref[j] = value + perturb * ground_ref[j].astype(F32)

    row = lax.broadcasted_iota(jnp.int32, (256, BANDS), 0)
    col = lax.broadcasted_iota(jnp.int32, (256, BANDS), 1)
    chip, member = row // 16, row % 8
    chip_x, chip_y = chip % 4, chip // 4
    natural = 32 * chip_x + 16 * (chip_y % 2) + 8 * (member // 4) + 4 * (chip_y // 2) + member % 4
    spread[...] = jnp.where(natural == col, 1.0, 0.0).astype(BF16)
    parity = (lax.broadcasted_iota(jnp.int32, (8, 256), 1) // 8) % 2

    for r in range(4):
        @pl.when(jnp.logical_not(mine(r)))
        def _():
            occ_out(r).wait_send()

    for_table(lambda i: table_copy(i).wait_send())
    for m in range(3):
        for_table(lambda i: table_on(i, m).wait_send())
    for h in range(2):
        for d in range(1, NZ):
            resp_copy(h, d).wait_send()
        sib_resp(h).wait_send()
        halo_copy(h).wait_send()
    occ_gather.finish()

    for s in range(16):
        resp_gather.wait_sib(s)

    def sib_exch(h):
        return remote(exch_wire.at[h], exch_sib.at[h], sib_s.at[2 + h], sib_r.at[2 + h], p.sibling)

    def sib_exch_start(h):
        exch_wire[h] = pack(jnp.concatenate([exch_own[2 * h], exch_own[2 * h + 1]], axis=0))
        sib_exch(h).start()

    reduce_finish(0)
    sib_exch_start(0)
    reduce_finish(1)
    sib_exch_start(1)

    zero = jnp.zeros((SLAB, N), F32)
    own_part = slab_of(lambda h: exch_wire[h])
    arrange(by_core(own_part, lambda r: zero))
    left_rows = rows32[...].reshape(N, N).astype(BF16)
    part = jnp.zeros((16, 256), F32)
    for a in range(SLAB // 2):
        bands = resp_all[:, a // 6, 16 * (a % 6) : 16 * (a % 6) + 16, :].reshape(256, N)
        part = part + lax.dot_general(
            left_rows[16 * a : 16 * a + 16],
            bands,
            (((1,), (1,)), ((), ())),
            preferred_element_type=F32,
        )
    folded = jnp.where(parity == 0, part[:8], part[8:])
    pieces = jnp.concatenate(split_bf16(folded), axis=0).astype(BF16)
    pieces = jnp.dot(pieces, spread[...], preferred_element_type=F32)
    gram_z[2 * z + c] = (pieces[:8] + pieces[8:16] + pieces[16:24]) * (1.0 / (N * N))

    z_line = [(d, k) for d in Z_ORDER for k in (0, 1)] + [(0, 1)]

    def line_core(k):
        return (1 - k) * c + k * (1 - c)

    def gram_copy(i):
        d, k = z_line[i]
        mine_slot = gram_z.at[2 * z + c]
        return remote(
            mine_slot, mine_slot, gz_s.at[i], gz_r.at[2 * z + c], p.z_peer(d, line_core(k))
        )

    for i in range(len(z_line)):
        gram_copy(i).start()

    for h in range(2):
        sib_exch(h).wait_recv()
    arrange(by_core(own_part, slab_of(lambda h: exch_sib[h])))
    exch_all[own, c] = rows_half()
    exch_gather.start()

    resp_gather.finish()
    for h in range(2):
        sib_exch(h).wait_send()
        for d in range(1, NZ):
            rs_copy(h, d).wait_send()

    for d, k in z_line:
        src = 2 * lax.rem(z + d, NZ) + line_core(k)
        slot = gram_z.at[src]
        remote(slot, slot, gz_s.at[0], gz_r.at[src], p.z_peer(d, line_core(k))).wait_recv()
    summed = gram_z[0]
    for i in range(1, 2 * NZ):
        summed = summed + gram_z[i]
    gram_xy[y, x] = summed

    def gram_plane(i):
        d, e = plane[i]
        slot = gram_xy.at[y, x]
        device = p.dev(mod4(x + d), mod4(y + e), z, c)
        return remote(slot, slot, gp_s.at[i], gp_r.at[own], device)

    for i in range(len(plane)):
        gram_plane(i).start()
    exch_gather.forward()
    exch_gather.hand_on(NEAR)
    for i in range(len(z_line)):
        gram_copy(i).wait_send()
    for d, e in plane:
        src_x, src_y = mod4(x + d), mod4(y + e)
        slot = gram_xy.at[src_y, src_x]
        remote(
            slot, slot, gp_s.at[0], gp_r.at[4 * src_y + src_x], p.dev(src_x, src_y, z, c)
        ).wait_recv()

    for i in range(32):
        n_x, n_lo, n_c, n_g = i // 8, (i // 4) % 2, (i // 2) % 2, i % 2
        gram_full[4 * i : 4 * i + 4, :] = gram_xy[2 * n_g + n_lo, n_x, 4 * n_c : 4 * n_c + 4, :]
    gram = gram_full[...]

    def halfway():
        exch_gather.hand_on(LATE)
        for i in range(len(plane)):
            gram_plane(i).wait_send()

    gram_full[...] = inverse_factor(0.5 * (gram + gram.T), halfway)
    inverse = gram_full[pl.ds(pl.multiple_of(8 * p.b, 8), 8), :]

    for s in range(16):
        exch_gather.wait_sib(s)

    for half in range(2):
        slot = 4 * (2 * half + p.y_lo) + x
        rows32[...] = exch_all[slot].reshape(SLAB, 8, N).astype(F32)
        for r in range(4):
            value = jnp.where(c == 0, rows32[:, r, :], rows32[:, 4 + r, :])
            res_ref[4 * half + r] = res_ref[4 * half + r] - EXCHANGE_FRACTION * value

    pieces = jnp.concatenate(split_bf16(inverse), axis=0).astype(BF16)
    wide = lax.dot_general(
        pieces, spread[...], (((1,), (1,)), ((), ())), preferred_element_type=F32
    )
    parity = jnp.concatenate([parity] * 3, axis=0)
    left = jnp.concatenate(
        [jnp.where(parity == 0, wide, 0.0), jnp.where(parity == 1, wide, 0.0)], axis=0
    ).astype(BF16)
    for a in range(SLAB // 2):
        vectors = exch_all[:, a // 6, 16 * (a % 6) : 16 * (a % 6) + 16, :].reshape(256, N)
        out = jnp.dot(left, vectors, preferred_element_type=F32)
        for k in range(2):
            o = out[24 * k : 24 * k + 24]
            proj32[:, 2 * a + k, :] = (o[16:24] + o[8:16]) + o[:8]
    for j in range(8):
        proj_ref[j] = proj32[j].astype(BF16)

    exch_gather.finish()


def on_device(*arguments):
    arguments = arguments[:7] + (arguments[7].T,)
    table = cosine_table(N)
    vmem = pl.BlockSpec(memory_space=pltpu.VMEM)
    hbm = pl.BlockSpec(memory_space=pltpu.HBM)
    dma = lambda n: pltpu.SemaphoreType.DMA((n,))
    scratch = [
        pltpu.VMEM((4, SLAB, N), BF16),
        pltpu.VMEM((8, SLAB, N), BF16),
        pltpu.VMEM((8, SLAB, N), BF16),
        pltpu.SMEM((8,), jnp.int32),
        pltpu.SMEM((8,), F32),
        pltpu.VMEM((SLAB, N), F32),
        pltpu.VMEM((3, SLAB, N), F32),
        pltpu.VMEM((N, N), BF16),
        pltpu.VMEM((N, N), BF16),
        pltpu.VMEM((4, WIRE_ONE, 128), BF16),
        pltpu.VMEM((4, WIRE_ONE, 128), BF16),
        pltpu.VMEM((NZ, WIRE, 128), BF16),
        pltpu.VMEM((NZ, WIRE - 16, 128), BF16),
        pltpu.VMEM((WIRE, 128), BF16),
        pltpu.VMEM((WIRE - 16, 128), BF16),
        pltpu.VMEM((2, WIRE, 128), BF16),
        pltpu.VMEM((4, N, N), BF16),
        pltpu.VMEM((NZ, SLAB, N), F32),
        pltpu.VMEM((N, N), F32),
        pltpu.VMEM((2, 8, N), F32),
        pltpu.VMEM((2, 8, N), F32),
        pltpu.VMEM((16, 2, 3 * HALF // 2, 128), BF16),
        pltpu.VMEM((16, N, N), BF16),
        pltpu.VMEM((16, 2, HALF, N), BF16),
        pltpu.VMEM((16, 2, HALF, N), BF16),
        pltpu.VMEM((4, N, N), F32),
        pltpu.VMEM((2, NZ, WIRE, 128), BF16),
        pltpu.VMEM((2, NZ, WIRE, 128), BF16),
        pltpu.VMEM((SLAB, 8, N), F32),
        pltpu.VMEM((4, SLAB, N), F32),
        pltpu.VMEM((2, WIRE, 128), BF16),
        pltpu.VMEM((2 * NZ, 8, BANDS), F32),
        pltpu.VMEM((4, 4, 8, BANDS), F32),
        pltpu.VMEM((BANDS, BANDS), F32),
        pltpu.VMEM((256, BANDS), BF16),
        pltpu.VMEM((8, SLAB, N), F32),
    ]
    counts = [10, 4, 4, 14, 16, 4, 4, 2, 8, 6, 2, 2, 14, 16, 15, 16, 15, 16] + [3, 12, 16, 16, 16] * 3
    scratch += [dma(n) for n in counts]
    return pl.pallas_call(
        kernel,
        out_shape=(pltpu.VMEM((8, SLAB, N), BF16), pltpu.VMEM((8, SLAB, N), F32)),
        in_specs=[hbm] * 10,
        out_specs=(vmem, vmem),
        scratch_shapes=scratch,
        compiler_params=pltpu.CompilerParams(
            collective_id=0, has_side_effects=True, vmem_limit_bytes=(64 << 20) - (10500 << 10)
        ),
        cost_estimate=pl.CostEstimate(
            flops=4 * 64 * 2 * N**3, bytes_accessed=4 << 20, transcendentals=0
        ),
    )(*arguments, jnp.asarray(table), jnp.asarray(np.ascontiguousarray(table.T)))


def solution(mesh):
    return jax.shard_map(
        on_device,
        mesh=mesh,
        in_specs=(
            P(("grp", "band"), "ga", None),
            P("band", "ga", None),
            P("band", "ga", None),
            P("band"),
            P("band"),
            P("ga", None),
            P(None, "ga", None),
            P(None, "ga"),
        ),
        out_specs=(P("band", "ga", None), P("band", "ga", None)),
        check_vma=False,
    )
```
